32 devices in a mesh: group: 2 (over y), depth: 4 (over z), plane: 2 (over x), batch: 2 (over core).
Axes of the slice: x: 2, y: 2, z: 4, core: 2. Of those that a mesh axis runs over, the one named last changes fastest.
Arguments:
- source: bfloat16 [4, 2, 32, 65536], P('depth', None, ('group', 'batch'), 'plane'), parts along dimension 2, may hold values from -6 to 6
- pool: bfloat16 [12, 3, 2, 256, 256], P('depth')
- near_mask: int32 [12, 256, 3], P('depth', 'plane'), may hold values 0 or 1
- layer_count: int32 [4], P('depth'), may hold values from 1 to 3, 8 in all
Outputs:
- up_top: bfloat16 [4, 2, 32, 65536], P('depth', None, ('group', 'batch'), 'plane'), parts along dimension 2
- down_bottom: bfloat16 [4, 2, 32, 65536], P('depth', None, ('group', 'batch'), 'plane'), parts along dimension 2
The draws below stay inside these ranges and needn't reach their ends.
There are 2 independent parts, one for each index of `group`. The reference program is written for one: setup_inputs(seed, part) draws one part's arguments, and reference() takes and returns one part's arrays. A program takes and returns all parts, laid end to end along the dimension named above; an argument that names none is the same for every part. Nothing has to cross between parts.
Inputs may be any that keep to these rules, and one draw needn't show every extreme that they name: `layer_count`: each section holds 1 to 3 layers, 8 in all; some section holds exactly 3.
All inputs are finite; a program needn't handle non-finite values. No bound on the sum of `near_mask` or of `layer_count` on one device may be relied on, other than what follows from the above.
Results may differ from the reference program's by a relative error of at most 0.012.
Values may be sent and summed in bfloat16 or wider, within the bound.
No kernel may reach another device: no remote copies, remote signals or barrier semaphores. Data moves between devices by JAX's collectives and lax.ppermute only.
A program may use at most 64 MiB of HBM per device.

```python
import math
import jax
import jax.numpy as jnp
import numpy as np
from jax import lax

M = 65536
BLK = 256
CAP = 3
B = 16
NB = 256
SLOTS = 12
LAYERS = 8
N_DEPTH = 4


def draw_pool(key, part):
    noise_key, phase_key = jax.random.split(jax.random.fold_in(key, 17))
    shape = (SLOTS, 3, 2, BLK, BLK)
    sigma = (0.2 / (6.0 * BLK)) ** 0.5
    noise = jax.random.normal(noise_key, shape, jnp.float32) * sigma
    radius = 0.85
    theta = jax.random.uniform(phase_key, (SLOTS, 1, 1, BLK, 1), jnp.float32, -math.pi, math.pi)
    phases = jnp.concatenate([jnp.cos(theta), jnp.sin(theta)], axis=2)
    places = jnp.arange(BLK)
    identity = (places[:, None] == places[None, :]).astype(jnp.float32)
    centre = (jnp.arange(3) == 1).astype(jnp.float32)[None, :, None, None, None]
    return (noise + radius * phases * identity * centre).astype(jnp.bfloat16)


def set_ends(result, rng, smallest, high):
    shape = result.shape
    spot = [jax.random.randint(jax.random.fold_in(rng, axis), (), 0, shape[axis]) for axis in range(len(shape))]
    result = result.at[tuple(spot)].set(smallest)
    longest = shape.index(max(shape))
    spot[longest] = (spot[longest] + 1) % shape[longest]
    return result.at[tuple(spot)].set(high)


def block_levels(stream_key, shape, cuts, least, top_value):
    level, own = 1.0, jax.random.fold_in(stream_key, 6)
    for position, parts in cuts:
        draws = jnp.exp(jax.random.uniform(jax.random.fold_in(own, position), (parts,), jnp.float32, least / len(cuts), top_value / len(cuts)))
        level = level * jnp.repeat(draws, shape[position] // parts).reshape([-1 if axis == position else 1 for axis in range(len(shape))])
    return level


def split_up(amount, total, most, lean):
    weights = [(1 << 20) // math.isqrt(grade ** lean) + 1 for grade in range(2, amount + 1)]
    surplus, holding = total - most - (amount - 1), [1] * (amount - 1)
    while surplus > 0:
        free = [i for i in range(amount - 1) if holding[i] < most]
        mass, left = sum([weights[i] for i in free]), surplus
        for i in free:
            more = min(most - holding[i], max(1, left * weights[i] // mass), surplus)
            holding[i] = holding[i] + more
            surplus = surplus - more
    return np.array([most] + holding)


def ragged_sizes(key, count, total, reach, skew):
    if count == 2:
        one = jax.random.randint(key, (), max(1, total - reach), min(reach, total - 1) + 1)
        return jnp.stack([one, total - one])
    lengths = jnp.asarray(split_up(count, total, reach, skew), jnp.int32)
    pairs = (count - 1) // 2
    giver, taker = lengths[1:1 + 2 * pairs:2], lengths[2:2 + 2 * pairs:2]
    room = jnp.minimum(giver - 1, reach - taker)
    passed = jax.random.randint(jax.random.fold_in(key, 1), (pairs,), 0, 1 << 20) % (room + 1)
    lengths = lengths.at[1:1 + 2 * pairs:2].set(giver - passed).at[2:2 + 2 * pairs:2].set(taker + passed)
    return lengths[jax.random.permutation(jax.random.fold_in(key, 2), count)]


def bell_draw(rng, shape, width, most, cuts=(), held_as=jnp.bfloat16):
    gain = block_levels(rng, shape, cuts, -0.22, 0.18) if cuts else 1.0
    entries = jax.random.normal(rng, shape, jnp.float32) * width * gain
    return jnp.minimum(jnp.maximum(entries, -most), most).astype(held_as)


def setup_inputs(seed: int = 0, part: int = 0) -> dict:
    seeds = jax.random.split(jax.random.key(seed), 5)
    own_keys = jax.random.split(jax.random.fold_in(seeds[4], part), 5)
    source = bell_draw(own_keys[0], (N_DEPTH, 2, B, M), 1.0, 6.0, ((0, 4), (2, 2), (3, 2)))
    pool = draw_pool(jax.random.fold_in(seeds[4], 71), part)
    near_mask = set_ends((jax.random.randint(seeds[2], (SLOTS, NB, 3), 0, 3) < 2).astype(jnp.int32), jax.random.fold_in(seeds[2], 1), 0, 1)
    layer_count = ragged_sizes(seeds[3], N_DEPTH, LAYERS, CAP, 1).astype(jnp.int32)
    return dict(source=source, pool=pool, near_mask=near_mask, layer_count=layer_count)


def apply_layer(trace, weights, present):
    padded = jnp.pad(trace, ((0, 0), (0, 0), (BLK, BLK)))
    total = jnp.zeros((2, B, NB, BLK), jnp.float32)
    for offset in range(3):
        segment = padded[:, :, offset * BLK: offset * BLK + M].reshape(2, B, NB, BLK).astype(jnp.float32)
        product = jnp.einsum("cbnq,kpq->ckbnp", segment, weights[offset].astype(jnp.float32))
        paired = jnp.stack([product[0, 0] - product[1, 1], product[1, 0] + product[0, 1]])
        if offset == 1:
            total = total + paired
        else:
            keep = present[:, offset].astype(jnp.float32)[None, None, :, None]
            total = total + paired * keep
    return total.reshape(2, B, M)


def reference(source, pool, near_mask, layer_count):
    stored = jnp.zeros((SLOTS, 2, B, M), jnp.bfloat16)
    bottoms = jnp.zeros((N_DEPTH, 2, B, M), jnp.bfloat16)
    tops = jnp.zeros((N_DEPTH, 2, B, M), jnp.bfloat16)

    def down_section(section, carry):
        trace, stored, bottoms = carry
        trace = (trace.astype(jnp.float32) + source[section].astype(jnp.float32)).astype(jnp.bfloat16)

        def layer_step(inner, state):
            trace, stored = state
            slot = section * CAP + inner
            stored = lax.dynamic_update_index_in_dim(stored, trace, slot, 0)
            weights = lax.dynamic_index_in_dim(pool, slot, 0, keepdims=False)
            present = lax.dynamic_index_in_dim(near_mask, slot, 0, keepdims=False)
            return apply_layer(trace, weights, present).astype(jnp.bfloat16), stored

        trace, stored = lax.fori_loop(0, layer_count[section], layer_step, (trace, stored))
        bottoms = lax.dynamic_update_index_in_dim(bottoms, trace, section, 0)
        return trace, stored, bottoms

    start = jnp.zeros((2, B, M), jnp.bfloat16)
    trace, stored, bottoms = lax.fori_loop(0, N_DEPTH, down_section, (start, stored, bottoms))

    def up_section(step, carry):
        trace, tops = carry
        section = N_DEPTH - 1 - step

        def layer_step(inner, trace):
            slot = section * CAP + layer_count[section] - 1 - inner
            weights = lax.dynamic_index_in_dim(pool, slot, 0, keepdims=False)
            present = lax.dynamic_index_in_dim(near_mask, slot, 0, keepdims=False)
            coupled = lax.dynamic_index_in_dim(stored, slot, 0, keepdims=False).astype(jnp.float32)
            return (apply_layer(trace, weights, present) + coupled).astype(jnp.bfloat16)

        trace = lax.fori_loop(0, layer_count[section], layer_step, trace)
        tops = lax.dynamic_update_index_in_dim(tops, trace, section, 0)
        return trace, tops

    trace, tops = lax.fori_loop(0, N_DEPTH, up_section, (start, tops))
    return tops, bottoms
```

```python
import functools

import jax
import jax.numpy as jnp
from jax import lax
from jax.experimental import pallas as pl
from jax.experimental.pallas import tpu as pltpu
from jax.sharding import PartitionSpec as P

NT = (((1,), (1,)), ((), ()))
CHUNKS = 4


def section_kernel(
    depth_n, chunks, sc, r1, r2, src, w, mask, state_in, top_in, bottom_in, o1, o2, state, top, bottom, up
):
    here, count, step = sc[0], sc[1], sc[2]
    rows = r1.shape[0]
    half = rows // 2
    window = mask.shape[2]
    down_at = step - here
    up_at = step - 2 * (depth_n - 1) + here
    down_due = (down_at >= 0) & (down_at < chunks)
    up_due = (up_at >= 0) & (up_at < chunks)
    even = lax.rem(here, 2) == 0
    odd = jnp.logical_not(even)

    def apply_layer(x, slot):
        wide = x.astype(jnp.float32)
        before = pltpu.roll(wide, 1, 0) * jnp.tile(mask[slot, 0], (rows // window, 2))
        after = pltpu.roll(wide, rows - 1, 0) * jnp.tile(mask[slot, 1], (rows // window, 2))
        total = lax.dot_general(before.astype(jnp.bfloat16), w[slot, 0], NT, preferred_element_type=jnp.float32)
        total = total + lax.dot_general(x, w[slot, 1], NT, preferred_element_type=jnp.float32)
        total = total + lax.dot_general(
            after.astype(jnp.bfloat16), w[slot, 2], NT, preferred_element_type=jnp.float32
        )
        block = total.shape[1] // 2
        real = total[:half, :block] - total[half:, block:]
        imag = total[half:, :block] + total[:half, block:]
        return real, imag

    @pl.when(down_due)
    def _():
        def enter(arrived):
            state[down_at, 0] = (
                arrived[...].astype(jnp.float32) + src[down_at].astype(jnp.float32)
            ).astype(jnp.bfloat16)

        pl.when(even)(lambda: enter(r2))
        pl.when(odd)(lambda: enter(r1))

        def layer(c, _):
            real, imag = apply_layer(state[down_at, c], c)
            state[down_at, c + 1, :half] = real.astype(jnp.bfloat16)
            state[down_at, c + 1, half:] = imag.astype(jnp.bfloat16)
            return 0

        lax.fori_loop(0, count, layer, 0)
        bottom[down_at] = state[down_at, count]

        @pl.when(even)
        def _():
            o1[...] = state[down_at, count]

        @pl.when(odd)
        def _():
            o2[...] = state[down_at, count]

    @pl.when(up_due)
    def _():
        @pl.when(even)
        def _():
            up[...] = r1[...]

        @pl.when(odd)
        def _():
            up[...] = r2[...]

        def layer(i, _):
            c = count - 1 - i
            real, imag = apply_layer(up[...], c)
            up[:half] = (real + state[up_at, c, :half].astype(jnp.float32)).astype(jnp.bfloat16)
            up[half:] = (imag + state[up_at, c, half:].astype(jnp.float32)).astype(jnp.bfloat16)
            return 0

        lax.fori_loop(0, count, layer, 0)
        top[up_at] = up[...]

        @pl.when(even)
        def _():
            o2[...] = up[...]

        @pl.when(odd)
        def _():
            o1[...] = up[...]


def section(depth_n, sc, r1, r2, src, w, mask, state, top, bottom):
    in_vmem = pl.BlockSpec(memory_space=pltpu.VMEM)
    held = lambda a: pltpu.with_memory_space_constraint(a, pltpu.VMEM)
    like = lambda a: pltpu.VMEM(a.shape, a.dtype)
    return pl.pallas_call(
        functools.partial(section_kernel, depth_n, src.shape[0]),
        out_shape=(like(r1), like(r2), like(state), like(top), like(bottom)),
        in_specs=[pl.BlockSpec(memory_space=pltpu.SMEM)] + [in_vmem] * 8,
        out_specs=(in_vmem,) * 5,
        scratch_shapes=[pltpu.VMEM(r1.shape, r1.dtype)],
        input_output_aliases={6: 2, 7: 3, 8: 4},
        compiler_params=pltpu.CompilerParams(vmem_limit_bytes=16 * 1024 * 1024),
    )(sc, *map(held, (r1, r2, src, w, mask, state, top, bottom)))


def windowed(cells, dim, tile, halo, start):
    planes = lax.axis_size("plane")
    if planes == 2:
        here = lax.axis_index("plane")
        tail = lax.slice_in_dim(cells, tile - halo, tile, axis=dim)
        head = lax.slice_in_dim(cells, 0, halo, axis=dim)
        arrived = lax.ppermute(jnp.where(here == 0, tail, head), "plane", [(0, 1), (1, 0)])
        first = jnp.concatenate([cells, arrived], axis=dim)
        second = jnp.concatenate([arrived, cells], axis=dim)
        return jnp.where(here == 0, first, second)
    whole = lax.all_gather(cells, "plane", axis=dim, tiled=True)
    size = min(whole.shape[dim], tile + 2 * halo)
    return lax.dynamic_slice_in_dim(whole, start, size, axis=dim)


def per_device(source, pool, near_mask, layer_count):
    depth_n = lax.axis_size("depth")
    planes = lax.axis_size("plane")
    here = lax.axis_index("depth")
    plane = lax.axis_index("plane")
    cap = pool.shape[0]
    block = pool.shape[-1]
    sources = source.shape[2]
    tile = source.shape[3] // block
    blocks = tile * planes
    halo = min(4 * depth_n, tile) if planes == 2 else 4 * depth_n
    window = tile + halo if planes == 2 else min(blocks, tile + 2 * halo)
    start = jnp.clip(plane * tile - halo, 0, blocks - window)
    own = plane * tile - start

    chunks = min(CHUNKS, sources)
    share = sources // chunks
    rows = 2 * share * window

    cells = windowed(source[0].reshape(2, sources, tile, block), 2, tile, halo, start)
    cells = cells.reshape(2, chunks, share, window, block).transpose(1, 0, 2, 3, 4)
    src = cells.reshape(chunks, rows, block)

    present = windowed(near_mask, 1, tile, halo, start).astype(jnp.float32)
    place = jnp.arange(window)[None, :]
    before = jnp.where(place == 0, 0.0, present[:, :, 0])
    after = jnp.where(place == window - 1, 0.0, present[:, :, 2])
    mask = jnp.broadcast_to(jnp.stack([before, after], axis=1)[..., None], (cap, 2, window, 128))
    w = pool.reshape(cap, 3, 2 * block, block)

    state = jnp.zeros((chunks, cap + 1, rows, block), jnp.bfloat16)
    top = jnp.zeros((chunks, rows, block), jnp.bfloat16)
    bottom = jnp.zeros((chunks, rows, block), jnp.bfloat16)
    r1 = jnp.zeros((rows, block), jnp.bfloat16)
    r2 = jnp.zeros((rows, block), jnp.bfloat16)

    def swaps(first):
        pairs = [(i, i + 1) for i in range(first, depth_n - 1, 2)]
        return pairs + [(j, i) for i, j in pairs]

    steps = chunks + 2 * (depth_n - 1)
    for step in range(steps):
        sc = jnp.stack([here, layer_count[0], jnp.int32(step)]).astype(jnp.int32)
        o1, o2, state, top, bottom = section(depth_n, sc, r1, r2, src, w, mask, state, top, bottom)
        if step < steps - 1:
            r1 = lax.ppermute(o1, "depth", swaps(0))
            if 0 < step < steps - 2:
                r2 = lax.ppermute(o2, "depth", swaps(1))

    def leave(held):
        held = held.reshape(chunks, 2, share, window, block)
        held = lax.dynamic_slice_in_dim(held, own, tile, axis=3)
        return held.transpose(1, 0, 2, 3, 4).reshape(1, 2, sources, tile * block)

    return (leave(top), leave(bottom))


def solution(mesh):
    return jax.shard_map(
        per_device,
        mesh=mesh,
        in_specs=(
            P("depth", None, ("group", "batch"), "plane"),
            P("depth", None, None, None, None),
            P("depth", "plane", None),
            P("depth"),
        ),
        out_specs=(
            P("depth", None, ("group", "batch"), "plane"),
            P("depth", None, ("group", "batch"), "plane"),
        ),
        check_vma=False,
    )
```

```python
import functools

import jax
import jax.numpy as jnp
from jax import lax
from jax.experimental import pallas as pl
from jax.experimental.pallas import tpu as pltpu
from jax.sharding import PartitionSpec as P

NT = (((1,), (1,)), ((), ()))
CHUNKS = 8
LAG = 2


def section_kernel(
    depth_n, chunks, sc, r1, r2, src, w, mask, state_in, top_in, bottom_in, o1, o2, state, top, bottom, up
):
    here, count, step = sc[0], sc[1], sc[2]
    rows = r1.shape[0]
    half = rows // 2
    window = mask.shape[2]
    down_at = step - LAG * here
    up_at = step - LAG * (2 * (depth_n - 1) - here)
    down_due = (down_at >= 0) & (down_at < chunks)
    up_due = (up_at >= 0) & (up_at < chunks)
    even = lax.rem(here, 2) == 0
    odd = jnp.logical_not(even)

    def apply_layer(x, slot):
        wide = x.astype(jnp.float32)
        before = pltpu.roll(wide, 1, 0) * jnp.tile(mask[slot, 0], (rows // window, 2))
        after = pltpu.roll(wide, rows - 1, 0) * jnp.tile(mask[slot, 1], (rows // window, 2))
        total = lax.dot_general(before.astype(jnp.bfloat16), w[slot, 0], NT, preferred_element_type=jnp.float32)
        total = total + lax.dot_general(x, w[slot, 1], NT, preferred_element_type=jnp.float32)
        total = total + lax.dot_general(
            after.astype(jnp.bfloat16), w[slot, 2], NT, preferred_element_type=jnp.float32
        )
        block = total.shape[1] // 2
        real = total[:half, :block] - total[half:, block:]
        imag = total[half:, :block] + total[:half, block:]
        return real, imag

    @pl.when(down_due)
    def _():
        def enter(arrived):
            state[down_at, 0] = (
                arrived[...].astype(jnp.float32) + src[down_at].astype(jnp.float32)
            ).astype(jnp.bfloat16)

        pl.when(even)(lambda: enter(r2))
        pl.when(odd)(lambda: enter(r1))

        def layer(c, _):
            real, imag = apply_layer(state[down_at, c], c)
            state[down_at, c + 1, :half] = real.astype(jnp.bfloat16)
            state[down_at, c + 1, half:] = imag.astype(jnp.bfloat16)
            return 0

        lax.fori_loop(0, count, layer, 0)
        bottom[down_at] = state[down_at, count]

        @pl.when(even)
        def _():
            o1[...] = state[down_at, count]

        @pl.when(odd)
        def _():
            o2[...] = state[down_at, count]

    @pl.when(up_due)
    def _():
        @pl.when(even)
        def _():
            up[...] = r1[...]

        @pl.when(odd)
        def _():
            up[...] = r2[...]

        def layer(i, _):
            c = count - 1 - i
            real, imag = apply_layer(up[...], c)
            up[:half] = (real + state[up_at, c, :half].astype(jnp.float32)).astype(jnp.bfloat16)
            up[half:] = (imag + state[up_at, c, half:].astype(jnp.float32)).astype(jnp.bfloat16)
            return 0

        lax.fori_loop(0, count, layer, 0)
        top[up_at] = up[...]

        @pl.when(even)
        def _():
            o2[...] = up[...]

        @pl.when(odd)
        def _():
            o1[...] = up[...]


def rows_of(a):
    return a.shape[0]


def section(depth_n, sc, r1, r2, src, w, mask, state, top, bottom):
    in_vmem = pl.BlockSpec(memory_space=pltpu.VMEM)
    held = lambda a: pltpu.with_memory_space_constraint(a, pltpu.VMEM)
    like = lambda a: pltpu.VMEM(a.shape, a.dtype)
    return pl.pallas_call(
        functools.partial(section_kernel, depth_n, src.shape[0]),
        out_shape=(like(r1), like(r2), like(state), like(top), like(bottom)),
        in_specs=[pl.BlockSpec(memory_space=pltpu.SMEM)] + [in_vmem] * 8,
        out_specs=(in_vmem,) * 5,
        scratch_shapes=[pltpu.VMEM(r1.shape, r1.dtype)],
        input_output_aliases={6: 2, 7: 3, 8: 4},
        compiler_params=pltpu.CompilerParams(vmem_limit_bytes=16 * 1024 * 1024),
        cost_estimate=pl.CostEstimate(flops=2 * 6 * 3 * 2 * rows_of(r1) * 256 * 256 * 2, bytes_accessed=1 << 20, transcendentals=0),
    )(sc, *map(held, (r1, r2, src, w, mask, state, top, bottom)))


def windowed(cells, dim, tile, halo, start):
    planes = lax.axis_size("plane")
    if planes == 2:
        here = lax.axis_index("plane")
        tail = lax.slice_in_dim(cells, tile - halo, tile, axis=dim)
        head = lax.slice_in_dim(cells, 0, halo, axis=dim)
        arrived = lax.ppermute(jnp.where(here == 0, tail, head), "plane", [(0, 1), (1, 0)])
        first = jnp.concatenate([cells, arrived], axis=dim)
        second = jnp.concatenate([arrived, cells], axis=dim)
        return jnp.where(here == 0, first, second)
    whole = lax.all_gather(cells, "plane", axis=dim, tiled=True)
    size = min(whole.shape[dim], tile + 2 * halo)
    return lax.dynamic_slice_in_dim(whole, start, size, axis=dim)


def per_device(source, pool, near_mask, layer_count):
    depth_n = lax.axis_size("depth")
    planes = lax.axis_size("plane")
    here = lax.axis_index("depth")
    plane = lax.axis_index("plane")
    cap = pool.shape[0]
    block = pool.shape[-1]
    sources = source.shape[2]
    tile = source.shape[3] // block
    blocks = tile * planes
    halo = min(4 * depth_n, tile) if planes == 2 else 4 * depth_n
    window = tile + halo if planes == 2 else min(blocks, tile + 2 * halo)
    start = jnp.clip(plane * tile - halo, 0, blocks - window)
    own = plane * tile - start

    chunks = min(CHUNKS, sources)
    share = sources // chunks
    rows = 2 * share * window

    cells = windowed(source[0].reshape(2, sources, tile, block), 2, tile, halo, start)
    cells = cells.reshape(2, chunks, share, window, block).transpose(1, 0, 2, 3, 4)
    src = cells.reshape(chunks, rows, block)

    present = windowed(near_mask, 1, tile, halo, start).astype(jnp.float32)
    place = jnp.arange(window)[None, :]
    before = jnp.where(place == 0, 0.0, present[:, :, 0])
    after = jnp.where(place == window - 1, 0.0, present[:, :, 2])
    mask = jnp.broadcast_to(jnp.stack([before, after], axis=1)[..., None], (cap, 2, window, 128))
    w = pool.reshape(cap, 3, 2 * block, block)

    state = jnp.zeros((chunks, cap + 1, rows, block), jnp.bfloat16)
    top = jnp.zeros((chunks, rows, block), jnp.bfloat16)
    bottom = jnp.zeros((chunks, rows, block), jnp.bfloat16)
    r1 = jnp.zeros((rows, block), jnp.bfloat16)
    r2 = jnp.zeros((rows, block), jnp.bfloat16)

    def swaps(first):
        pairs = [(i, i + 1) for i in range(first, depth_n - 1, 2)]
        return pairs + [(j, i) for i, j in pairs]

    steps = chunks + 2 * LAG * (depth_n - 1)
    queue = [(r1, r2)] * LAG
    for step in range(steps):
        sc = jnp.stack([here, layer_count[0], jnp.int32(step)]).astype(jnp.int32)
        r1, r2 = queue.pop(0)
        o1, o2, state, top, bottom = section(depth_n, sc, r1, r2, src, w, mask, state, top, bottom)
        if step < steps - LAG:
            n1 = lax.ppermute(o1, "depth", swaps(0))
            n2 = lax.ppermute(o2, "depth", swaps(1)) if LAG <= step < steps - 2 * LAG else r2
            queue.append((n1, n2))

    def leave(held):
        held = held.reshape(chunks, 2, share, window, block)
        held = lax.dynamic_slice_in_dim(held, own, tile, axis=3)
        return held.transpose(1, 0, 2, 3, 4).reshape(1, 2, sources, tile * block)

    return (leave(top), leave(bottom))


def solution(mesh):
    return jax.shard_map(
        per_device,
        mesh=mesh,
        in_specs=(
            P("depth", None, ("group", "batch"), "plane"),
            P("depth", None, None, None, None),
            P("depth", "plane", None),
            P("depth"),
        ),
        out_specs=(
            P("depth", None, ("group", "batch"), "plane"),
            P("depth", None, ("group", "batch"), "plane"),
        ),
        check_vma=False,
    )
```

```python
import functools

import jax
import jax.numpy as jnp
from jax import lax
from jax.experimental import pallas as pl
from jax.experimental.pallas import tpu as pltpu
from jax.sharding import PartitionSpec as P

NT = (((1,), (1,)), ((), ()))
CHUNKS = 8
LAG = 2
VMEM_LIMIT = 16 * 1024 * 1024


def apply_layer(x, w, mask, slot):
    rows, window = x.shape[0], mask.shape[2]
    half = rows // 2
    wide = x.astype(jnp.float32)
    before = pltpu.roll(wide, 1, 0) * jnp.tile(mask[slot, 0], (rows // window, 2))
    after = pltpu.roll(wide, rows - 1, 0) * jnp.tile(mask[slot, 1], (rows // window, 2))
    total = lax.dot_general(before.astype(jnp.bfloat16), w[slot, 0], NT, preferred_element_type=jnp.float32)
    total = total + lax.dot_general(x, w[slot, 1], NT, preferred_element_type=jnp.float32)
    total = total + lax.dot_general(after.astype(jnp.bfloat16), w[slot, 2], NT, preferred_element_type=jnp.float32)
    block = total.shape[1] // 2
    real = total[:half, :block] - total[half:, block:]
    imag = total[half:, :block] + total[:half, block:]
    return real, imag


def section_kernel(depth_n, chunks, step, plan, *refs):
    refs = dict(zip(plan, refs))
    sc, src, w, mask, state = (refs[name] for name in ("sc", "src", "w", "mask", "state"))
    here, count = sc[0], sc[1]
    down_at = step - LAG * here
    up_at = step - LAG * (2 * (depth_n - 1) - here)
    even = lax.rem(here, 2) == 0
    odd = jnp.logical_not(even)
    half = src.shape[1] // 2

    def choose(first, second, then):
        pl.when(even)(lambda: then(refs.get(first)))
        pl.when(odd)(lambda: then(refs.get(second)))

    def down():
        def enter(arrived):
            x = src[down_at]
            if arrived is not None:
                x = (arrived[...].astype(jnp.float32) + x.astype(jnp.float32)).astype(jnp.bfloat16)
            state[down_at, 0] = x

        choose("r2", "r1", enter)

        def layer(c, _):
            real, imag = apply_layer(state[down_at, c], w, mask, c)
            state[down_at, c + 1, :half] = real.astype(jnp.bfloat16)
            state[down_at, c + 1, half:] = imag.astype(jnp.bfloat16)
            return 0

        lax.fori_loop(0, count, layer, 0)
        refs["bottom"][down_at] = state[down_at, count]

        def send(out):
            if out is not None:
                out[...] = state[down_at, count]

        choose("o1", "o2", send)

    def rise():
        up = refs["up"]

        def enter(arrived):
            up[...] = jnp.zeros_like(up) if arrived is None else arrived[...]

        choose("r1", "r2", enter)

        def layer(i, _):
            c = count - 1 - i
            real, imag = apply_layer(up[...], w, mask, c)
            up[:half] = (real + state[up_at, c, :half].astype(jnp.float32)).astype(jnp.bfloat16)
            up[half:] = (imag + state[up_at, c, half:].astype(jnp.float32)).astype(jnp.bfloat16)
            return 0

        lax.fori_loop(0, count, layer, 0)
        refs["top"][up_at] = up[...]

        def send(out):
            if out is not None:
                out[...] = up[...]

        choose("o2", "o1", send)

    if "bottom" in refs:
        pl.when((down_at >= 0) & (down_at < chunks))(down)
    if "top" in refs:
        pl.when((up_at >= 0) & (up_at < chunks))(rise)


def held(a):
    return pltpu.with_memory_space_constraint(a, pltpu.VMEM)


def section(depth_n, step, sc, fixed, arrived, kept, sends):
    src = fixed["src"]
    chunks, rows, block = src.shape
    cap = fixed["w"].shape[0]
    in_vmem = pl.BlockSpec(memory_space=pltpu.VMEM)
    shapes = {"state": (chunks, cap + 1, rows, block), "bottom": src.shape, "top": src.shape}
    writes = ["state"] * ("bottom" in kept) + [name for name in ("bottom", "top") if name in kept]
    ins = {**fixed, **arrived, **{name: a for name, a in kept.items() if a is not None}}
    outs = writes + list(sends)
    aliases = {1 + list(ins).index(name): outs.index(name) for name in writes if name in ins}
    plan = ["sc"] + list(ins) + outs + ["up"]
    results = pl.pallas_call(
        functools.partial(section_kernel, depth_n, chunks, step, plan),
        out_shape=tuple(pltpu.VMEM(shapes.get(name, (rows, block)), src.dtype) for name in outs),
        in_specs=[pl.BlockSpec(memory_space=pltpu.SMEM)] + [in_vmem] * len(ins),
        out_specs=(in_vmem,) * len(outs),
        scratch_shapes=[pltpu.VMEM((rows, block), src.dtype)],
        input_output_aliases=aliases,
        compiler_params=pltpu.CompilerParams(vmem_limit_bytes=VMEM_LIMIT),
        cost_estimate=pl.CostEstimate(
            flops=12 * rows * 6 * block * block, bytes_accessed=8 * rows * block, transcendentals=0
        ),
    )(pltpu.with_memory_space_constraint(sc, pltpu.SMEM), *map(held, ins.values()))
    return dict(zip(outs, results))


LANES = 128


def enter_kernel(source, pool, own_mask, sc, src, mask, w, natural, wide, sems):
    own = pl.multiple_of(sc[2], 16)
    bring = pltpu.make_async_copy(pool, w, sems.at[0])
    load = pltpu.make_async_copy(source, natural, sems.at[1])
    load.start()
    bring.start()
    sources, window = src.shape[0], wide.shape[2] // src.shape[0]
    tile = own_mask.shape[0]
    cap = mask.shape[0]
    columns = own_mask[...].astype(jnp.float32)
    for slot in range(cap):
        for side in range(2):
            at = slot * 3 + 2 * side
            mask[slot, side, pl.ds(own, tile), :] = jnp.broadcast_to(columns[:, at : at + 1], (tile, LANES))
    load.wait()
    spread(natural, wide, own, tile, sources, window)
    for part in range(2):
        for s in range(sources):
            for h in range(2):
                src[s, pl.ds(part * window + own, tile), h * LANES : (h + 1) * LANES] = wide[
                    part, h, pl.ds(s * window + own, tile), :
                ].astype(src.dtype)
    bring.wait()


def spread(natural, wide, first, count, sources, window):
    def block(n, _):
        for part in range(2):
            for h in range(2):
                lanes = pl.ds(pl.multiple_of((2 * n + h) * LANES, LANES), LANES)
                wide[part, h, pl.ds(first + n, sources, stride=window), :] = natural[part, :, lanes].astype(jnp.float32)
        return 0

    lax.fori_loop(0, count, block, 0, unroll=4)


def join_kernel(arrived, sc, src_in, mask_in, src, mask, wide):
    own = sc[2]
    sources, window = src.shape[0], wide.shape[2] // src.shape[0]
    cap = mask.shape[0]
    halo = arrived.shape[2] // (2 * LANES)
    at = pl.multiple_of(jnp.where(own == 0, window - halo, 0), 16)
    spread(arrived, wide, at, halo, sources, window)
    for part in range(2):
        for s in range(sources):
            for h in range(2):
                src[s, pl.ds(part * window + at, halo), h * LANES : (h + 1) * LANES] = wide[
                    part, h, pl.ds(s * window + at, halo), :
                ].astype(src.dtype)
    columns = arrived[:, :, 2 * halo * LANES :].astype(jnp.float32).reshape(-1, LANES)[:halo]
    place = lax.broadcasted_iota(jnp.int32, (window, LANES), 0)
    for slot in range(cap):
        for side in range(2):
            j = slot * 3 + 2 * side
            mask[slot, side, pl.ds(at, halo), :] = jnp.broadcast_to(
                columns[:, j : j + 1], (halo, LANES)
            )
            end = 0 if side == 0 else window - 1
            mask[slot, side] = jnp.where(place == end, 0.0, mask[slot, side])


def leave_kernel(result, sc, out, wide, natural, sem):
    own = sc[2]
    sources, window = result.shape[0], result.shape[1] // 2
    tile = out.shape[2] // (2 * LANES)
    for part in range(2):
        for s in range(sources):
            for h in range(2):
                wide[part, h, pl.ds(s * window, window), :] = result[
                    s, pl.ds(part * window, window), h * LANES : (h + 1) * LANES
                ].astype(jnp.float32)

    def block(n, _):
        for part in range(2):
            for h in range(2):
                lanes = pl.ds(pl.multiple_of((2 * n + h) * LANES, LANES), LANES)
                natural[part, :, lanes] = wide[part, h, pl.ds(own + n, sources, stride=window), :].astype(out.dtype)
        return 0

    lax.fori_loop(0, tile, block, 0, unroll=4)
    copy = pltpu.make_async_copy(natural, out, sem)
    copy.start()
    copy.wait()


IN_VMEM = pl.BlockSpec(memory_space=pltpu.VMEM)
IN_SMEM = pl.BlockSpec(memory_space=pltpu.SMEM)
IN_HBM = pl.BlockSpec(memory_space=pltpu.HBM)


def in_smem(a):
    return pltpu.with_memory_space_constraint(a, pltpu.SMEM)


def cost(size):
    return pl.CostEstimate(flops=0, bytes_accessed=size, transcendentals=0)


def per_device(source, pool, near_mask, layer_count):
    depth_n = lax.axis_size("depth")
    planes = lax.axis_size("plane")
    here = lax.axis_index("depth")
    plane = lax.axis_index("plane")
    cap = pool.shape[0]
    block = pool.shape[-1]
    sources = source.shape[2]
    tile = source.shape[3] // block
    blocks = tile * planes
    halo = min(4 * depth_n, tile) if planes == 2 else 4 * depth_n
    window = tile + halo if planes == 2 else min(blocks, tile + 2 * halo)
    start = jnp.clip(plane * tile - halo, 0, blocks - window)
    own = plane * tile - start
    chunks = sources
    rows = 2 * window
    params = pltpu.CompilerParams(vmem_limit_bytes=VMEM_LIMIT)
    bf16, f32 = jnp.bfloat16, jnp.float32

    sc = jnp.stack([here, layer_count[0], own]).astype(jnp.int32)
    cells = source[0]
    weights = pool.reshape(cap, 3, 2 * block, block)
    wide = pltpu.VMEM((2, 2, sources * window, LANES), f32)
    if planes == 2:
        columns = near_mask.transpose(1, 0, 2).reshape(tile, cap * 3).astype(bf16)
        columns = jnp.pad(columns, ((0, 0), (0, LANES - cap * 3)))
        sent = jnp.where(
            plane == 0,
            jnp.concatenate([cells[:, :, (tile - halo) * block :], beside(columns[tile - halo :], sources)], axis=2),
            jnp.concatenate([cells[:, :, : halo * block], beside(columns[:halo], sources)], axis=2),
        )
        arrived = lax.ppermute(sent, "plane", [(0, 1), (1, 0)])
        src, mask, w = pl.pallas_call(
            enter_kernel,
            out_shape=(
                pltpu.VMEM((chunks, rows, block), bf16),
                pltpu.VMEM((cap, 2, window, LANES), f32),
                pltpu.VMEM(weights.shape, bf16),
            ),
            in_specs=[IN_HBM, IN_HBM, IN_VMEM, IN_SMEM],
            out_specs=(IN_VMEM,) * 3,
            scratch_shapes=[pltpu.VMEM(cells.shape, bf16), wide, pltpu.SemaphoreType.DMA((2,))],
            compiler_params=params,
            cost_estimate=cost(1 << 23),
        )(cells, weights, columns, in_smem(sc))
        src, mask = pl.pallas_call(
            join_kernel,
            out_shape=(pltpu.VMEM(src.shape, bf16), pltpu.VMEM(mask.shape, f32)),
            in_specs=[IN_VMEM, IN_SMEM, IN_VMEM, IN_VMEM],
            out_specs=(IN_VMEM,) * 2,
            input_output_aliases={2: 0, 3: 1},
            scratch_shapes=[wide],
            compiler_params=params,
            cost_estimate=cost(1 << 20),
        )(held(arrived), in_smem(sc), held(src), held(mask))
    else:
        whole = lax.all_gather(cells, "plane", axis=2, tiled=True)
        src = lax.dynamic_slice_in_dim(whole, start * block, window * block, axis=2)
        src = src.reshape(2, sources, window, block).transpose(1, 0, 2, 3).reshape(chunks, rows, block)
        present = lax.all_gather(near_mask, "plane", axis=1, tiled=True)
        present = lax.dynamic_slice_in_dim(present, start, window, axis=1).astype(f32)
        place = jnp.arange(window)[None, :]
        before = jnp.where(place == 0, 0.0, present[:, :, 0])
        after = jnp.where(place == window - 1, 0.0, present[:, :, 2])
        mask = jnp.broadcast_to(jnp.stack([before, after], axis=1)[..., None], (cap, 2, window, LANES))
        w = weights

    def swaps(first):
        pairs = [(i, i + 1) for i in range(first, depth_n - 1, 2)]
        return pairs + [(j, i) for i, j in pairs]

    last_down = chunks + LAG * (depth_n - 1)
    first_up = LAG * (depth_n - 1)
    steps = chunks + 2 * LAG * (depth_n - 1)
    queue = [{}] * LAG
    kept = {}
    for step in range(steps):
        sends = {}
        if step < steps - LAG:
            sends["o1"] = ("r1", swaps(0))
        if LAG <= step < steps - 2 * LAG:
            sends["o2"] = ("r2", swaps(1))
        held_now = {"state": kept.get("state")}
        if step < last_down:
            held_now["bottom"] = kept.get("bottom")
        if step >= first_up:
            held_now["top"] = kept.get("top")
        out = section(depth_n, step, sc, dict(src=src, w=w, mask=mask), queue.pop(0), held_now, sends)
        queue.append({to: lax.ppermute(out.pop(name), "depth", pairs) for name, (to, pairs) in sends.items()})
        kept.update(out)

    def leave(result):
        return pl.pallas_call(
            leave_kernel,
            out_shape=jax.ShapeDtypeStruct(cells.shape, bf16),
            in_specs=[IN_VMEM, IN_SMEM],
            out_specs=IN_HBM,
            scratch_shapes=[wide, pltpu.VMEM(cells.shape, bf16), pltpu.SemaphoreType.DMA],
            compiler_params=params,
            cost_estimate=cost(1 << 23),
        )(held(result), in_smem(sc))[None]

    return (leave(kept["top"]), leave(kept["bottom"]))


def beside(columns, sources):
    lines = 2 * sources
    folds = -(-columns.shape[0] // lines)
    columns = jnp.pad(columns, ((0, folds * lines - columns.shape[0]), (0, 0)))
    return columns.reshape(folds, 2, sources, LANES).transpose(1, 2, 0, 3).reshape(2, sources, folds * LANES)


def solution(mesh):
    return jax.shard_map(
        per_device,
        mesh=mesh,
        in_specs=(
            P("depth", None, ("group", "batch"), "plane"),
            P("depth", None, None, None, None),
            P("depth", "plane", None),
            P("depth"),
        ),
        out_specs=(
            P("depth", None, ("group", "batch"), "plane"),
            P("depth", None, ("group", "batch"), "plane"),
        ),
        check_vma=False,
    )
```

```python
import functools

import jax
import jax.numpy as jnp
from jax import lax
from jax.experimental import pallas as pl
from jax.experimental.pallas import tpu as pltpu
from jax.sharding import PartitionSpec as P

NT = (((1,), (1,)), ((), ()))
CHUNKS = 8
LAG = 2
VMEM_LIMIT = 16 * 1024 * 1024


def apply_layer(x, w, mask, slot):
    rows, window = x.shape[0], mask.shape[2]
    half = rows // 2
    wide = x.astype(jnp.float32)
    before = pltpu.roll(wide, 1, 0) * jnp.tile(mask[slot, 0], (rows // window, 2))
    after = pltpu.roll(wide, rows - 1, 0) * jnp.tile(mask[slot, 1], (rows // window, 2))
    total = lax.dot_general(before.astype(jnp.bfloat16), w[slot, 0], NT, preferred_element_type=jnp.float32)
    total = total + lax.dot_general(x, w[slot, 1], NT, preferred_element_type=jnp.float32)
    total = total + lax.dot_general(after.astype(jnp.bfloat16), w[slot, 2], NT, preferred_element_type=jnp.float32)
    block = total.shape[1] // 2
    real = total[:half, :block] - total[half:, block:]
    imag = total[half:, :block] + total[:half, block:]
    return real, imag


def section_kernel(depth_n, chunks, step, plan, *refs):
    refs = dict(zip(plan, refs))
    sc, src, w, mask, state = (refs[name] for name in ("sc", "src", "w", "mask", "state"))
    here, count = sc[0], sc[1]
    down_at = step - LAG * here
    up_at = step - LAG * (2 * (depth_n - 1) - here)
    even = lax.rem(here, 2) == 0
    odd = jnp.logical_not(even)
    half = src.shape[1] // 2

    def choose(first, second, then):
        pl.when(even)(lambda: then(refs.get(first)))
        pl.when(odd)(lambda: then(refs.get(second)))

    def down():
        def enter(arrived):
            x = src[down_at]
            if arrived is None:
                state[down_at, 0] = x
                return

            @pl.when(here == 0)
            def _():
                state[down_at, 0] = x

            @pl.when(here > 0)
            def _():
                state[down_at, 0] = (arrived[...].astype(jnp.float32) + x.astype(jnp.float32)).astype(jnp.bfloat16)

        choose("r2", "r1", enter)

        def layer(c, _):
            real, imag = apply_layer(state[down_at, c], w, mask, c)
            state[down_at, c + 1, :half] = real.astype(jnp.bfloat16)
            state[down_at, c + 1, half:] = imag.astype(jnp.bfloat16)
            return 0

        lax.fori_loop(0, count, layer, 0)
        refs["bottom"][down_at] = state[down_at, count]

        def send(out):
            if out is not None:
                out[...] = state[down_at, count]

        choose("o1", "o2", send)

    def rise():
        up = refs["up"]

        def enter(arrived):
            if arrived is not None:

                @pl.when(here < depth_n - 1)
                def _():
                    up[...] = arrived[...]

            @pl.when(here == depth_n - 1)
            def _():
                up[...] = jnp.zeros_like(up)

        choose("r1", "r2", enter)

        def layer(i, _):
            c = count - 1 - i
            real, imag = apply_layer(up[...], w, mask, c)
            up[:half] = (real + state[up_at, c, :half].astype(jnp.float32)).astype(jnp.bfloat16)
            up[half:] = (imag + state[up_at, c, half:].astype(jnp.float32)).astype(jnp.bfloat16)
            return 0

        lax.fori_loop(0, count, layer, 0)
        refs["top"][up_at] = up[...]

        def send(out):
            if out is not None:
                out[...] = up[...]

        choose("o2", "o1", send)

    if "bottom" in refs:
        pl.when((down_at >= 0) & (down_at < chunks))(down)
    if "top" in refs:
        pl.when((up_at >= 0) & (up_at < chunks))(rise)


def held(a):
    return pltpu.with_memory_space_constraint(a, pltpu.VMEM)


def section(depth_n, step, sc, fixed, arrived, kept, sends):
    src = fixed["src"]
    chunks, rows, block = src.shape
    cap = fixed["w"].shape[0]
    in_vmem = pl.BlockSpec(memory_space=pltpu.VMEM)
    shapes = {"state": (chunks, cap + 1, rows, block), "bottom": src.shape, "top": src.shape}
    writes = ["state"] * ("bottom" in kept) + [name for name in ("bottom", "top") if name in kept]
    ins = {**fixed, **arrived, **{name: a for name, a in kept.items() if a is not None}}
    outs = writes + list(sends)
    aliases = {1 + list(ins).index(name): outs.index(name) for name in writes if name in ins}
    plan = ["sc"] + list(ins) + outs + ["up"]
    results = pl.pallas_call(
        functools.partial(section_kernel, depth_n, chunks, step, plan),
        out_shape=tuple(pltpu.VMEM(shapes.get(name, (rows, block)), src.dtype) for name in outs),
        in_specs=[pl.BlockSpec(memory_space=pltpu.SMEM)] + [in_vmem] * len(ins),
        out_specs=(in_vmem,) * len(outs),
        scratch_shapes=[pltpu.VMEM((rows, block), src.dtype)],
        input_output_aliases=aliases,
        compiler_params=pltpu.CompilerParams(vmem_limit_bytes=VMEM_LIMIT),
        cost_estimate=pl.CostEstimate(
            flops=12 * rows * 6 * block * block, bytes_accessed=8 * rows * block, transcendentals=0
        ),
    )(pltpu.with_memory_space_constraint(sc, pltpu.SMEM), *map(held, ins.values()))
    return dict(zip(outs, results))


LANES = 128


def enter_kernel(source, pool, own_mask, sc, src, mask, w, natural, wide, sems):
    own = pl.multiple_of(sc[2], 16)
    bring = pltpu.make_async_copy(pool, w, sems.at[0])
    load = pltpu.make_async_copy(source, natural, sems.at[1])
    load.start()
    bring.start()
    sources, window = src.shape[0], wide.shape[2] // src.shape[0]
    tile = own_mask.shape[0]
    cap = mask.shape[0]
    columns = own_mask[...].astype(jnp.float32)
    for slot in range(cap):
        for side in range(2):
            at = slot * 3 + 2 * side
            mask[slot, side, pl.ds(own, tile), :] = jnp.broadcast_to(columns[:, at : at + 1], (tile, LANES))
    load.wait()
    spread(natural, wide, own, tile, sources, window)
    for part in range(2):
        for s in range(sources):
            for h in range(2):
                src[s, pl.ds(part * window + own, tile), h * LANES : (h + 1) * LANES] = wide[
                    part, h, pl.ds(s * window + own, tile), :
                ].astype(src.dtype)
    bring.wait()


def spread(natural, wide, first, count, sources, window):
    def block(n, _):
        for part in range(2):
            for h in range(2):
                lanes = pl.ds(pl.multiple_of((2 * n + h) * LANES, LANES), LANES)
                wide[part, h, pl.ds(first + n, sources, stride=window), :] = natural[part, :, lanes].astype(jnp.float32)
        return 0

    lax.fori_loop(0, count, block, 0, unroll=4)


def join_kernel(arrived, sc, src_in, mask_in, src, mask, wide):
    own = sc[2]
    sources, window = src.shape[0], wide.shape[2] // src.shape[0]
    cap = mask.shape[0]
    halo = arrived.shape[2] // (2 * LANES)
    at = pl.multiple_of(jnp.where(own == 0, window - halo, 0), 16)
    spread(arrived, wide, at, halo, sources, window)
    for part in range(2):
        for s in range(sources):
            for h in range(2):
                src[s, pl.ds(part * window + at, halo), h * LANES : (h + 1) * LANES] = wide[
                    part, h, pl.ds(s * window + at, halo), :
                ].astype(src.dtype)
    columns = arrived[:, :, 2 * halo * LANES :].astype(jnp.float32).reshape(-1, LANES)[:halo]
    place = lax.broadcasted_iota(jnp.int32, (window, LANES), 0)
    for slot in range(cap):
        for side in range(2):
            j = slot * 3 + 2 * side
            mask[slot, side, pl.ds(at, halo), :] = jnp.broadcast_to(
                columns[:, j : j + 1], (halo, LANES)
            )
            end = 0 if side == 0 else window - 1
            mask[slot, side] = jnp.where(place == end, 0.0, mask[slot, side])


def leave_kernel(result, sc, out, wide, natural, sem):
    own = sc[2]
    sources, window = result.shape[0], result.shape[1] // 2
    tile = out.shape[2] // (2 * LANES)
    for part in range(2):
        for s in range(sources):
            for h in range(2):
                wide[part, h, pl.ds(s * window, window), :] = result[
                    s, pl.ds(part * window, window), h * LANES : (h + 1) * LANES
                ].astype(jnp.float32)

    def block(n, _):
        for part in range(2):
            for h in range(2):
                lanes = pl.ds(pl.multiple_of((2 * n + h) * LANES, LANES), LANES)
                natural[part, :, lanes] = wide[part, h, pl.ds(own + n, sources, stride=window), :].astype(out.dtype)
        return 0

    lax.fori_loop(0, tile, block, 0, unroll=4)
    copy = pltpu.make_async_copy(natural, out, sem)
    copy.start()
    copy.wait()


def scalars_kernel(facts, sc):
    for i in range(sc.shape[0]):
        sc[i] = facts[i, 0]


IN_VMEM = pl.BlockSpec(memory_space=pltpu.VMEM)
IN_SMEM = pl.BlockSpec(memory_space=pltpu.SMEM)
IN_HBM = pl.BlockSpec(memory_space=pltpu.HBM)


def in_smem(a):
    return pltpu.with_memory_space_constraint(a, pltpu.SMEM)


def cost(size):
    return pl.CostEstimate(flops=0, bytes_accessed=size, transcendentals=0)


def per_device(source, pool, near_mask, layer_count):
    depth_n = lax.axis_size("depth")
    planes = lax.axis_size("plane")
    here = lax.axis_index("depth")
    plane = lax.axis_index("plane")
    cores = lax.axis_size("batch")
    cap = pool.shape[0]
    block = pool.shape[-1]
    sources = source.shape[2]
    tile = source.shape[3] // block
    blocks = tile * planes
    halo = min(4 * depth_n, tile) if planes == 2 else 4 * depth_n
    window = tile + halo if planes == 2 else min(blocks, tile + 2 * halo)
    start = jnp.clip(plane * tile - halo, 0, blocks - window)
    own = plane * tile - start
    chunks = sources
    rows = 2 * window
    params = pltpu.CompilerParams(vmem_limit_bytes=VMEM_LIMIT)
    bf16, f32 = jnp.bfloat16, jnp.float32

    facts = jnp.stack([here, layer_count[0], own]).astype(jnp.int32)
    facts = jnp.broadcast_to(jnp.pad(facts, (0, 5))[:, None], (8, LANES))
    sc = pl.pallas_call(
        scalars_kernel,
        out_shape=pltpu.SMEM((3,), jnp.int32),
        in_specs=[IN_VMEM],
        out_specs=IN_SMEM,
    )(held(facts))
    cells = source[0]
    weights = pool.reshape(cap, 3, 2 * block, block)
    wide = pltpu.VMEM((2, 2, sources * window, LANES), f32)
    if planes == 2:
        columns = near_mask.transpose(1, 0, 2).reshape(tile, cap * 3).astype(bf16)
        columns = jnp.pad(columns, ((0, 0), (0, LANES - cap * 3)))
        sent = jnp.where(
            plane == 0,
            jnp.concatenate([cells[:, :, (tile - halo) * block :], beside(columns[tile - halo :], sources)], axis=2),
            jnp.concatenate([cells[:, :, : halo * block], beside(columns[:halo], sources)], axis=2),
        )
        arrived = lax.ppermute(sent, "plane", [(0, 1), (1, 0)])
        src, mask, w = pl.pallas_call(
            enter_kernel,
            out_shape=(
                pltpu.VMEM((chunks, rows, block), bf16),
                pltpu.VMEM((cap, 2, window, LANES), f32),
                pltpu.VMEM(weights.shape, bf16),
            ),
            in_specs=[IN_HBM, IN_HBM, IN_VMEM, IN_SMEM],
            out_specs=(IN_VMEM,) * 3,
            scratch_shapes=[pltpu.VMEM(cells.shape, bf16), wide, pltpu.SemaphoreType.DMA((2,))],
            compiler_params=params,
            cost_estimate=cost(1 << 23),
        )(cells, weights, columns, in_smem(sc))
        src, mask = pl.pallas_call(
            join_kernel,
            out_shape=(pltpu.VMEM(src.shape, bf16), pltpu.VMEM(mask.shape, f32)),
            in_specs=[IN_VMEM, IN_SMEM, IN_VMEM, IN_VMEM],
            out_specs=(IN_VMEM,) * 2,
            input_output_aliases={2: 0, 3: 1},
            scratch_shapes=[wide],
            compiler_params=params,
            cost_estimate=cost(1 << 20),
        )(held(arrived), in_smem(sc), held(src), held(mask))
    else:
        whole = lax.all_gather(cells, "plane", axis=2, tiled=True)
        src = lax.dynamic_slice_in_dim(whole, start * block, window * block, axis=2)
        src = src.reshape(2, sources, window, block).transpose(1, 0, 2, 3).reshape(chunks, rows, block)
        present = lax.all_gather(near_mask, "plane", axis=1, tiled=True)
        present = lax.dynamic_slice_in_dim(present, start, window, axis=1).astype(f32)
        place = jnp.arange(window)[None, :]
        before = jnp.where(place == 0, 0.0, present[:, :, 0])
        after = jnp.where(place == window - 1, 0.0, present[:, :, 2])
        mask = jnp.broadcast_to(jnp.stack([before, after], axis=1)[..., None], (cap, 2, window, LANES))
        w = weights

    def swaps(first):
        pairs = [(i, i + 1) for i in range(first, depth_n - 1, 2)]
        alone = sorted(set(range(depth_n)) - {i for pair in pairs for i in pair})
        moves = [(i * cores + c, j * cores + c) for i, j in pairs for c in range(cores)]
        moves += [(i * cores + c, i * cores + c + 1) for i in alone for c in range(0, cores - 1, 2)]
        return moves + [(j, i) for i, j in moves]

    last_down = chunks + LAG * (depth_n - 1)
    first_up = LAG * (depth_n - 1)
    steps = chunks + 2 * LAG * (depth_n - 1)
    queue = [{}] * LAG
    kept = {}
    for step in range(steps):
        sends = {}
        if step < steps - LAG:
            sends["o1"] = ("r1", swaps(0))
        if LAG <= step < steps - 2 * LAG:
            sends["o2"] = ("r2", swaps(1))
        held_now = {"state": kept.get("state")}
        if step < last_down:
            held_now["bottom"] = kept.get("bottom")
        if step >= first_up:
            held_now["top"] = kept.get("top")
        out = section(depth_n, step, sc, dict(src=src, w=w, mask=mask), queue.pop(0), held_now, sends)
        queue.append({to: lax.ppermute(out.pop(name), ("depth", "batch"), pairs) for name, (to, pairs) in sends.items()})
        kept.update(out)

    def leave(result):
        return pl.pallas_call(
            leave_kernel,
            out_shape=jax.ShapeDtypeStruct(cells.shape, bf16),
            in_specs=[IN_VMEM, IN_SMEM],
            out_specs=IN_HBM,
            scratch_shapes=[wide, pltpu.VMEM(cells.shape, bf16), pltpu.SemaphoreType.DMA],
            compiler_params=params,
            cost_estimate=cost(1 << 23),
        )(held(result), in_smem(sc))[None]

    return (leave(kept["top"]), leave(kept["bottom"]))


def beside(columns, sources):
    lines = 2 * sources
    folds = -(-columns.shape[0] // lines)
    columns = jnp.pad(columns, ((0, folds * lines - columns.shape[0]), (0, 0)))
    return columns.reshape(folds, 2, sources, LANES).transpose(1, 2, 0, 3).reshape(2, sources, folds * LANES)


def solution(mesh):
    return jax.shard_map(
        per_device,
        mesh=mesh,
        in_specs=(
            P("depth", None, ("group", "batch"), "plane"),
            P("depth", None, None, None, None),
            P("depth", "plane", None),
            P("depth"),
        ),
        out_specs=(
            P("depth", None, ("group", "batch"), "plane"),
            P("depth", None, ("group", "batch"), "plane"),
        ),
        check_vma=False,
    )
```

```python
import functools

import jax
import jax.numpy as jnp
from jax import lax
from jax.experimental import pallas as pl
from jax.experimental.pallas import tpu as pltpu
from jax.sharding import PartitionSpec as P

NN = (((1,), (0,)), ((), ()))
CHUNKS = 8
LAG = 2
VMEM_LIMIT = 16 * 1024 * 1024


def apply_layer(x, w, mask, slot):
    rows, window = x.shape[0], mask.shape[2]
    half = rows // 2
    wide = x.astype(jnp.float32)
    before = pltpu.roll(wide, 1, 0) * jnp.tile(mask[slot, 0], (rows // window, 2))
    after = pltpu.roll(wide, rows - 1, 0) * jnp.tile(mask[slot, 1], (rows // window, 2))
    total = lax.dot_general(before.astype(jnp.bfloat16), w[slot, 0], NN, preferred_element_type=jnp.float32)
    total = total + lax.dot_general(x, w[slot, 1], NN, preferred_element_type=jnp.float32)
    total = total + lax.dot_general(after.astype(jnp.bfloat16), w[slot, 2], NN, preferred_element_type=jnp.float32)
    block = total.shape[1] // 2
    real = total[:half, :block] - total[half:, block:]
    imag = total[half:, :block] + total[:half, block:]
    return real, imag


def section_kernel(depth_n, chunks, step, plan, *refs):
    refs = dict(zip(plan, refs))
    sc, src, w, mask, state = (refs[name] for name in ("sc", "src", "w", "mask", "state"))
    here, count = sc[0], sc[1]
    down_at = step - LAG * here
    up_at = step - LAG * (2 * (depth_n - 1) - here)
    even = lax.rem(here, 2) == 0
    odd = jnp.logical_not(even)
    half = src.shape[1] // 2

    def choose(first, second, then):
        pl.when(even)(lambda: then(refs.get(first)))
        pl.when(odd)(lambda: then(refs.get(second)))

    def down():
        def enter(arrived):
            x = src[down_at]
            if arrived is None:
                state[down_at, 0] = x
                return

            @pl.when(here == 0)
            def _():
                state[down_at, 0] = x

            @pl.when(here > 0)
            def _():
                state[down_at, 0] = (arrived[...].astype(jnp.float32) + x.astype(jnp.float32)).astype(jnp.bfloat16)

        choose("r2", "r1", enter)

        def layer(c, _):
            real, imag = apply_layer(state[down_at, c], w, mask, c)
            state[down_at, c + 1, :half] = real.astype(jnp.bfloat16)
            state[down_at, c + 1, half:] = imag.astype(jnp.bfloat16)
            return 0

        lax.fori_loop(0, count, layer, 0)
        refs["bottom"][down_at] = state[down_at, count]

        def send(out):
            if out is not None:
                out[...] = state[down_at, count]

        choose("o1", "o2", send)

    def rise():
        up = refs["up"]

        def enter(arrived):
            if arrived is not None:

                @pl.when(here < depth_n - 1)
                def _():
                    up[...] = arrived[...]

            @pl.when(here == depth_n - 1)
            def _():
                up[...] = jnp.zeros_like(up)

        choose("r1", "r2", enter)

        def layer(i, _):
            c = count - 1 - i
            real, imag = apply_layer(up[...], w, mask, c)
            up[:half] = (real + state[up_at, c, :half].astype(jnp.float32)).astype(jnp.bfloat16)
            up[half:] = (imag + state[up_at, c, half:].astype(jnp.float32)).astype(jnp.bfloat16)
            return 0

        lax.fori_loop(0, count, layer, 0)
        refs["top"][up_at] = up[...]

        def send(out):
            if out is not None:
                out[...] = up[...]

        choose("o2", "o1", send)

    if "bottom" in refs:
        pl.when((down_at >= 0) & (down_at < chunks))(down)
    if "top" in refs:
        pl.when((up_at >= 0) & (up_at < chunks))(rise)


def held(a):
    return pltpu.with_memory_space_constraint(a, pltpu.VMEM)


def section(depth_n, step, sc, fixed, arrived, kept, sends):
    src = fixed["src"]
    chunks, rows, block = src.shape
    cap = fixed["w"].shape[0]
    in_vmem = pl.BlockSpec(memory_space=pltpu.VMEM)
    shapes = {"state": (chunks, cap + 1, rows, block), "bottom": src.shape, "top": src.shape}
    writes = ["state"] * ("bottom" in kept) + [name for name in ("bottom", "top") if name in kept]
    ins = {**fixed, **arrived, **{name: a for name, a in kept.items() if a is not None}}
    outs = writes + list(sends)
    aliases = {1 + list(ins).index(name): outs.index(name) for name in writes if name in ins}
    plan = ["sc"] + list(ins) + outs + ["up"]
    results = pl.pallas_call(
        functools.partial(section_kernel, depth_n, chunks, step, plan),
        out_shape=tuple(pltpu.VMEM(shapes.get(name, (rows, block)), src.dtype) for name in outs),
        in_specs=[pl.BlockSpec(memory_space=pltpu.SMEM)] + [in_vmem] * len(ins),
        out_specs=(in_vmem,) * len(outs),
        scratch_shapes=[pltpu.VMEM((rows, block), src.dtype)],
        input_output_aliases=aliases,
        compiler_params=pltpu.CompilerParams(vmem_limit_bytes=VMEM_LIMIT),
        cost_estimate=pl.CostEstimate(
            flops=12 * rows * 6 * block * block, bytes_accessed=8 * rows * block, transcendentals=0
        ),
    )(pltpu.with_memory_space_constraint(sc, pltpu.SMEM), *map(held, ins.values()))
    return dict(zip(outs, results))


LANES = 128


def offer_kernel(source, near, facts, payload, sc, lines, sem):
    for i in range(sc.shape[0]):
        sc[i] = facts[i, 0]
    sources, width = payload.shape[1], payload.shape[2] - LANES
    first = jnp.where(facts[2, 0] == 0, source.shape[2] - width, 0)
    copy = pltpu.make_async_copy(
        source.at[:, :, pl.ds(pl.multiple_of(first, LANES), width)], payload.at[:, :, pl.ds(0, width)], sem
    )
    copy.start()
    lines[...] = jnp.zeros_like(lines)
    for slot in range(near.shape[0]):
        for side in range(2):
            at = slot * 2 + side
            lines[at : at + 1, :] = near[slot, 2 * side : 2 * side + 1, :].astype(jnp.float32)
    for part in range(2):
        payload[part, :, width:] = lines[part * sources : (part + 1) * sources].astype(payload.dtype)
    copy.wait()


def column(line):
    return jnp.broadcast_to(line, (LANES, LANES)).T


def enter_kernel(source, pool, near, sc, src, mask, w, natural, wide, raw, sems):
    own = pl.multiple_of(sc[2], 16)
    bring = pltpu.make_async_copy(pool, raw, sems.at[0])
    load = pltpu.make_async_copy(source, natural, sems.at[1])
    load.start()
    bring.start()
    sources = src.shape[0]
    window = mask.shape[2]
    tile = near.shape[2]
    for slot in range(mask.shape[0]):
        for side in range(2):
            mask[slot, side, pl.ds(own, tile), :] = column(near[slot, 2 * side : 2 * side + 1, :].astype(jnp.float32))
    load.wait()
    spread(natural, wide, own, tile, sources, window)
    for part in range(2):
        for s in range(sources):
            for h in range(2):
                src[s, pl.ds(part * window + own, tile), h * LANES : (h + 1) * LANES] = wide[
                    part, h, pl.ds(s * (window + 1) + own, tile), :
                ].astype(src.dtype)
    bring.wait()

    def turn(i, _):
        slot, offset = i // 3, lax.rem(i, 3)
        w[slot, offset] = raw[slot, offset].T
        return 0

    lax.fori_loop(0, raw.shape[0] * 3, turn, 0)


def spread(natural, wide, first, count, sources, window):
    def block(n, _):
        for part in range(2):
            for h in range(2):
                lanes = pl.ds(pl.multiple_of((2 * n + h) * LANES, LANES), LANES)
                wide[part, h, pl.ds(first + n, sources, stride=window + 1), :] = natural[part, :, lanes].astype(
                    jnp.float32
                )
        return 0

    lax.fori_loop(0, count, block, 0, unroll=8)


def join_kernel(arrived, sc, src_in, mask_in, src, mask, wide):
    own = sc[2]
    sources, window = src.shape[0], mask.shape[2]
    halo = arrived.shape[2] // (2 * LANES)
    width = 2 * halo * LANES
    at = pl.multiple_of(jnp.where(own == 0, window - halo, 0), 16)
    spread(arrived, wide, at, halo, sources, window)
    for part in range(2):
        for s in range(sources):
            for h in range(2):
                src[s, pl.ds(part * window + at, halo), h * LANES : (h + 1) * LANES] = wide[
                    part, h, pl.ds(s * (window + 1) + at, halo), :
                ].astype(src.dtype)
    for slot in range(mask.shape[0]):
        for side in range(2):
            r = slot * 2 + side
            line = arrived[r // sources, r % sources : r % sources + 1, width:].astype(jnp.float32)
            rows = column(line)
            mask[slot, side, pl.ds(at, halo), :] = jnp.where(own == 0, rows[:halo], rows[LANES - halo :])
            end = 0 if side == 0 else window - 1
            mask[slot, side, end : end + 1, :] = jnp.zeros((1, LANES), jnp.float32)


PIECES = 4


def leave_kernel(result, sc, out, wide, natural, sems):
    own = sc[2]
    sources, window = result.shape[0], result.shape[1] // 2
    tile = out.shape[2] // (2 * LANES)
    stride = window + 1
    for part in range(2):
        for s in range(sources):
            for h in range(2):
                wide[part, h, pl.ds(s * stride, window), :] = result[
                    s, pl.ds(part * window, window), h * LANES : (h + 1) * LANES
                ].astype(jnp.float32)

    def block(n, _):
        for part in range(2):
            for h in range(2):
                lanes = pl.ds(pl.multiple_of((2 * n + h) * LANES, LANES), LANES)
                natural[part, :, lanes] = wide[part, h, pl.ds(own + n, sources, stride=stride), :].astype(out.dtype)
        return 0

    pieces = PIECES if tile % PIECES == 0 else 1
    each = tile // pieces
    copies = []
    for piece in range(pieces):
        lax.fori_loop(piece * each, (piece + 1) * each, block, 0, unroll=8)
        lanes = pl.ds(piece * each * 2 * LANES, each * 2 * LANES)
        copies.append(pltpu.make_async_copy(natural.at[:, :, lanes], out.at[:, :, lanes], sems.at[piece]))
        copies[-1].start()
    for copy in copies:
        copy.wait()


def scalars_kernel(facts, sc):
    for i in range(sc.shape[0]):
        sc[i] = facts[i, 0]


IN_VMEM = pl.BlockSpec(memory_space=pltpu.VMEM)
IN_SMEM = pl.BlockSpec(memory_space=pltpu.SMEM)
IN_HBM = pl.BlockSpec(memory_space=pltpu.HBM)


def in_smem(a):
    return pltpu.with_memory_space_constraint(a, pltpu.SMEM)


def cost(size):
    return pl.CostEstimate(flops=0, bytes_accessed=size, transcendentals=0)


def per_device(source, pool, near_mask, layer_count):
    depth_n = lax.axis_size("depth")
    planes = lax.axis_size("plane")
    here = lax.axis_index("depth")
    plane = lax.axis_index("plane")
    cores = lax.axis_size("batch")
    cap = pool.shape[0]
    block = pool.shape[-1]
    sources = source.shape[2]
    tile = source.shape[3] // block
    blocks = tile * planes
    halo = min(4 * depth_n, tile) if planes == 2 else 4 * depth_n
    window = tile + halo if planes == 2 else min(blocks, tile + 2 * halo)
    start = jnp.clip(plane * tile - halo, 0, blocks - window)
    own = plane * tile - start
    chunks = sources
    rows = 2 * window
    params = pltpu.CompilerParams(vmem_limit_bytes=VMEM_LIMIT)
    bf16, f32 = jnp.bfloat16, jnp.float32

    facts = jnp.stack([here, layer_count[0], own]).astype(jnp.int32)
    facts = jnp.broadcast_to(jnp.pad(facts, (0, 5))[:, None], (8, LANES))
    cells = pltpu.with_memory_space_constraint(source[0], pltpu.HBM)
    weights = pltpu.with_memory_space_constraint(pool.reshape(cap, 3, 2 * block, block), pltpu.HBM)
    wide = pltpu.VMEM((2, 2, sources * (window + 1) + 8, LANES), f32)
    scalars = pltpu.SMEM((3,), jnp.int32)
    if planes == 2 and tile == LANES and 2 * cap <= sources:
        near = near_mask.transpose(0, 2, 1)
        payload, sc = pl.pallas_call(
            offer_kernel,
            out_shape=(pltpu.VMEM((2, sources, halo * block + LANES), bf16), scalars),
            in_specs=[IN_HBM, IN_VMEM, IN_VMEM],
            out_specs=(IN_VMEM, IN_SMEM),
            scratch_shapes=[pltpu.VMEM((2 * sources, LANES), f32), pltpu.SemaphoreType.DMA],
            compiler_params=params,
            cost_estimate=cost(1 << 20),
        )(cells, held(near), held(facts))
        arrived = lax.ppermute(payload, "plane", [(0, 1), (1, 0)])
        src, mask, w = pl.pallas_call(
            enter_kernel,
            out_shape=(
                pltpu.VMEM((chunks, rows, block), bf16),
                pltpu.VMEM((cap, 2, window, LANES), f32),
                pltpu.VMEM((cap, 3, block, 2 * block), bf16),
            ),
            in_specs=[IN_HBM, IN_HBM, IN_VMEM, IN_SMEM],
            out_specs=(IN_VMEM,) * 3,
            scratch_shapes=[
                pltpu.VMEM(source.shape[1:], bf16), wide, pltpu.VMEM(weights.shape, bf16), pltpu.SemaphoreType.DMA((2,))
            ],
            compiler_params=params,
            cost_estimate=cost(1 << 23),
        )(cells, weights, held(near), in_smem(sc))
        src, mask = pl.pallas_call(
            join_kernel,
            out_shape=(pltpu.VMEM(src.shape, bf16), pltpu.VMEM(mask.shape, f32)),
            in_specs=[IN_VMEM, IN_SMEM, IN_VMEM, IN_VMEM],
            out_specs=(IN_VMEM,) * 2,
            input_output_aliases={2: 0, 3: 1},
            scratch_shapes=[wide],
            compiler_params=params,
            cost_estimate=cost(1 << 20),
        )(held(arrived), in_smem(sc), held(src), held(mask))
    else:
        sc = pl.pallas_call(scalars_kernel, out_shape=scalars, in_specs=[IN_VMEM], out_specs=IN_SMEM)(held(facts))
        whole = lax.all_gather(source[0], "plane", axis=2, tiled=True)
        src = lax.dynamic_slice_in_dim(whole, start * block, window * block, axis=2)
        src = src.reshape(2, sources, window, block).transpose(1, 0, 2, 3).reshape(chunks, rows, block)
        present = lax.all_gather(near_mask, "plane", axis=1, tiled=True)
        present = lax.dynamic_slice_in_dim(present, start, window, axis=1).astype(f32)
        place = jnp.arange(window)[None, :]
        before = jnp.where(place == 0, 0.0, present[:, :, 0])
        after = jnp.where(place == window - 1, 0.0, present[:, :, 2])
        mask = jnp.broadcast_to(jnp.stack([before, after], axis=1)[..., None], (cap, 2, window, LANES))
        w = pool.reshape(cap, 3, 2 * block, block).swapaxes(2, 3)

    def swaps(first):
        pairs = [(i, i + 1) for i in range(first, depth_n - 1, 2)]
        alone = sorted(set(range(depth_n)) - {i for pair in pairs for i in pair})
        moves = [(i * cores + c, j * cores + c) for i, j in pairs for c in range(cores)]
        moves += [(i * cores + c, i * cores + c + 1) for i in alone for c in range(0, cores - 1, 2)]
        return moves + [(j, i) for i, j in moves]

    last_down = chunks + LAG * (depth_n - 1)
    first_up = LAG * (depth_n - 1)
    steps = chunks + 2 * LAG * (depth_n - 1)
    queue = [{}] * LAG
    kept = {}

    def leave(result):
        return pl.pallas_call(
            leave_kernel,
            out_shape=jax.ShapeDtypeStruct(source.shape[1:], bf16),
            in_specs=[IN_VMEM, IN_SMEM],
            out_specs=IN_HBM,
            scratch_shapes=[wide, pltpu.VMEM(source.shape[1:], bf16), pltpu.SemaphoreType.DMA((PIECES,))],
            compiler_params=params,
            cost_estimate=cost(1 << 22),
        )(held(result), in_smem(sc))[None]

    for step in range(steps):
        if step == steps - 1:
            kept["bottom"], kept["top"] = lax.optimization_barrier((kept["bottom"], kept["top"]))
            bottom = leave(kept["bottom"])
            bottom, kept["top"] = lax.optimization_barrier((bottom, kept["top"]))
        sends = {}
        if step < steps - LAG:
            sends["o1"] = ("r1", swaps(0))
        if LAG <= step < steps - 2 * LAG:
            sends["o2"] = ("r2", swaps(1))
        held_now = {"state": kept.get("state")}
        if step < last_down:
            held_now["bottom"] = kept.get("bottom")
        if step >= first_up:
            held_now["top"] = kept.get("top")
        out = section(depth_n, step, sc, dict(src=src, w=w, mask=mask), queue.pop(0), held_now, sends)
        queue.append({to: lax.ppermute(out.pop(name), ("depth", "batch"), pairs) for name, (to, pairs) in sends.items()})
        kept.update(out)

    return (leave(kept["top"]), bottom)


def solution(mesh):
    return jax.shard_map(
        per_device,
        mesh=mesh,
        in_specs=(
            P("depth", None, ("group", "batch"), "plane"),
            P("depth", None, None, None, None),
            P("depth", "plane", None),
            P("depth"),
        ),
        out_specs=(
            P("depth", None, ("group", "batch"), "plane"),
            P("depth", None, ("group", "batch"), "plane"),
        ),
        check_vma=False,
    )
```

```python
import functools

import jax
import jax.numpy as jnp
from jax import lax
from jax.experimental import pallas as pl
from jax.experimental.pallas import tpu as pltpu
from jax.sharding import PartitionSpec as P

NN = (((1,), (0,)), ((), ()))
NT = (((1,), (1,)), ((), ()))
CHUNKS = 8
LAG = 2
VMEM_LIMIT = 16 * 1024 * 1024


def apply_layer(x, w, mask, slot):
    rows, window = x.shape[0], mask.shape[2]
    half = rows // 2
    how = NN if w.shape[2] < w.shape[3] else NT
    wide = x.astype(jnp.float32)
    before = pltpu.roll(wide, 1, 0) * jnp.tile(mask[slot, 0], (rows // window, 2))
    after = pltpu.roll(wide, rows - 1, 0) * jnp.tile(mask[slot, 1], (rows // window, 2))
    total = lax.dot_general(before.astype(jnp.bfloat16), w[slot, 0], how, preferred_element_type=jnp.float32)
    total = total + lax.dot_general(x, w[slot, 1], how, preferred_element_type=jnp.float32)
    total = total + lax.dot_general(after.astype(jnp.bfloat16), w[slot, 2], how, preferred_element_type=jnp.float32)
    block = total.shape[1] // 2
    real = total[:half, :block] - total[half:, block:]
    imag = total[half:, :block] + total[:half, block:]
    return real, imag


def section_kernel(depth_n, chunks, step, plan, *refs):
    refs = dict(zip(plan, refs))
    sc, src, w, mask, state = (refs[name] for name in ("sc", "src", "w", "mask", "state"))
    here, count = sc[0], sc[1]
    down_at = step - LAG * here
    up_at = step - LAG * (2 * (depth_n - 1) - here)
    even = lax.rem(here, 2) == 0
    odd = jnp.logical_not(even)
    half = src.shape[1] // 2

    def choose(first, second, then):
        pl.when(even)(lambda: then(refs.get(first)))
        pl.when(odd)(lambda: then(refs.get(second)))

    def down():
        def enter(arrived):
            x = src[down_at]
            if arrived is None:
                state[down_at, 0] = x
                return

            @pl.when(here == 0)
            def _():
                state[down_at, 0] = x

            @pl.when(here > 0)
            def _():
                state[down_at, 0] = (arrived[...].astype(jnp.float32) + x.astype(jnp.float32)).astype(jnp.bfloat16)

        choose("r2", "r1", enter)

        def layer(c, _):
            real, imag = apply_layer(state[down_at, c], w, mask, c)
            state[down_at, c + 1, :half] = real.astype(jnp.bfloat16)
            state[down_at, c + 1, half:] = imag.astype(jnp.bfloat16)
            return 0

        lax.fori_loop(0, count, layer, 0)
        refs["bottom"][down_at] = state[down_at, count]

        def send(out):
            if out is not None:
                out[...] = state[down_at, count]

        choose("o1", "o2", send)

    def rise():
        up = refs["up"]

        def enter(arrived):
            if arrived is not None:

                @pl.when(here < depth_n - 1)
                def _():
                    up[...] = arrived[...]

            @pl.when(here == depth_n - 1)
            def _():
                up[...] = jnp.zeros_like(up)

        choose("r1", "r2", enter)

        def layer(i, _):
            c = count - 1 - i
            real, imag = apply_layer(up[...], w, mask, c)
            up[:half] = (real + state[up_at, c, :half].astype(jnp.float32)).astype(jnp.bfloat16)
            up[half:] = (imag + state[up_at, c, half:].astype(jnp.float32)).astype(jnp.bfloat16)
            return 0

        lax.fori_loop(0, count, layer, 0)
        refs["top"][up_at] = up[...]

        def send(out):
            if out is not None:
                out[...] = up[...]

        choose("o2", "o1", send)

    if "bottom" in refs:
        pl.when((down_at >= 0) & (down_at < chunks))(down)
    if "top" in refs:
        pl.when((up_at >= 0) & (up_at < chunks))(rise)


def held(a):
    return pltpu.with_memory_space_constraint(a, pltpu.VMEM)


def section(depth_n, step, sc, fixed, arrived, kept, sends):
    src = fixed["src"]
    chunks, rows, block = src.shape
    cap = fixed["w"].shape[0]
    in_vmem = pl.BlockSpec(memory_space=pltpu.VMEM)
    shapes = {"state": (chunks, cap + 1, rows, block), "bottom": src.shape, "top": src.shape}
    writes = ["state"] * ("bottom" in kept) + [name for name in ("bottom", "top") if name in kept]
    ins = {**fixed, **arrived, **{name: a for name, a in kept.items() if a is not None}}
    outs = writes + list(sends)
    aliases = {1 + list(ins).index(name): outs.index(name) for name in writes if name in ins}
    plan = ["sc"] + list(ins) + outs + ["up"]
    results = pl.pallas_call(
        functools.partial(section_kernel, depth_n, chunks, step, plan),
        out_shape=tuple(pltpu.VMEM(shapes.get(name, (rows, block)), src.dtype) for name in outs),
        in_specs=[pl.BlockSpec(memory_space=pltpu.SMEM)] + [in_vmem] * len(ins),
        out_specs=(in_vmem,) * len(outs),
        scratch_shapes=[pltpu.VMEM((rows, block), src.dtype)],
        input_output_aliases=aliases,
        compiler_params=pltpu.CompilerParams(vmem_limit_bytes=VMEM_LIMIT),
        cost_estimate=pl.CostEstimate(
            flops=12 * rows * 6 * block * block, bytes_accessed=8 * rows * block, transcendentals=0
        ),
    )(pltpu.with_memory_space_constraint(sc, pltpu.SMEM), *map(held, ins.values()))
    return dict(zip(outs, results))


LANES = 128


def offer_kernel(source, near, facts, head, payload, sc, near_out, lines, sems):
    for i in range(sc.shape[0]):
        sc[i] = facts[i, 0]
    width = payload.shape[2]
    halo = width // (2 * LANES)
    first = jnp.where(facts[2, 0] == 0, source.shape[2] - width, 0)
    copy = pltpu.make_async_copy(source.at[:, :, pl.ds(pl.multiple_of(first, LANES), width)], payload, sems.at[0])
    bring = pltpu.make_async_copy(near, near_out, sems.at[1])
    copy.start()
    bring.start()
    lines[...] = jnp.zeros_like(lines)
    bring.wait()
    for slot in range(near.shape[0]):
        for side in range(2):
            at = 2 * halo + slot * 2 + side
            lines[at : at + 1, :LANES] = near_out[slot, 2 * side : 2 * side + 1, :].astype(jnp.float32)
    copy.wait()
    for part in range(2):
        for n in range(halo):
            at = part * halo + n
            lines[at : at + 1, :] = payload[part, 0:1, 2 * n * LANES : 2 * (n + 1) * LANES].astype(jnp.float32)
    head[...] = lines[...].astype(head.dtype)


def column(line):
    return jnp.broadcast_to(line, (LANES, LANES)).T


def enter_kernel(source, pool, near, sc, src, mask, w, natural, wide, sems):
    own = pl.multiple_of(sc[2], 16)
    bring = pltpu.make_async_copy(pool, w, sems.at[0])
    load = pltpu.make_async_copy(source, natural, sems.at[1])
    load.start()
    bring.start()
    sources = src.shape[0]
    window = mask.shape[2]
    tile = near.shape[2]
    for slot in range(mask.shape[0]):
        for side in range(2):
            mask[slot, side, pl.ds(own, tile), :] = column(near[slot, 2 * side : 2 * side + 1, :].astype(jnp.float32))
    load.wait()
    spread(natural, wide, own, tile, sources, window)
    for part in range(2):
        for s in range(sources):
            for h in range(2):
                src[s, pl.ds(part * window + own, tile), h * LANES : (h + 1) * LANES] = wide[
                    part, h, pl.ds(s * (window + 1) + own, tile), :
                ].astype(src.dtype)
    bring.wait()


def turn_kernel(w, turned):
    def turn(i, _):
        slot, offset = i // 3, lax.rem(i, 3)
        turned[slot, offset] = w[slot, offset].T
        return 0

    lax.fori_loop(0, w.shape[0] * 3, turn, 0)


def spread(natural, wide, first, count, sources, window):
    def block(n, _):
        for part in range(2):
            for h in range(2):
                lanes = pl.ds(pl.multiple_of((2 * n + h) * LANES, LANES), LANES)
                wide[part, h, pl.ds(first + n, sources, stride=window + 1), :] = natural[part, :, lanes].astype(
                    jnp.float32
                )
        return 0

    lax.fori_loop(0, count, block, 0, unroll=8)


def join_head_kernel(head, sc, src_in, mask_in, src, mask):
    own = sc[2]
    window = mask.shape[2]
    halo = (head.shape[0] - 16) // 2
    at = pl.multiple_of(jnp.where(own == 0, window - halo, 0), 16)
    for part in range(2):
        src[0, pl.ds(part * window + at, halo), :] = head[part * halo : (part + 1) * halo, :]
    for slot in range(mask.shape[0]):
        for side in range(2):
            r = 2 * halo + slot * 2 + side
            rows = column(head[r : r + 1, :LANES].astype(jnp.float32))
            mask[slot, side, pl.ds(at, halo), :] = jnp.where(own == 0, rows[:halo], rows[LANES - halo :])
            end = 0 if side == 0 else window - 1
            mask[slot, side, end : end + 1, :] = jnp.zeros((1, LANES), jnp.float32)


def join_kernel(arrived, sc, src_in, src, wide):
    own = sc[2]
    sources, window = src.shape[0], src.shape[1] // 2
    halo = arrived.shape[2] // (2 * LANES)
    at = pl.multiple_of(jnp.where(own == 0, window - halo, 0), 16)
    spread(arrived, wide, at, halo, sources, window)
    for part in range(2):
        for s in range(1, sources):
            for h in range(2):
                src[s, pl.ds(part * window + at, halo), h * LANES : (h + 1) * LANES] = wide[
                    part, h, pl.ds(s * (window + 1) + at, halo), :
                ].astype(src.dtype)


PIECES = 4


def leave_kernel(result, sc, out, wide, natural, sems):
    own = sc[2]
    sources, window = result.shape[0], result.shape[1] // 2
    tile = out.shape[2] // (2 * LANES)
    stride = window + 1
    for part in range(2):
        for s in range(sources):
            for h in range(2):
                wide[part, h, pl.ds(s * stride, window), :] = result[
                    s, pl.ds(part * window, window), h * LANES : (h + 1) * LANES
                ].astype(jnp.float32)

    def block(n, _):
        for part in range(2):
            for h in range(2):
                lanes = pl.ds(pl.multiple_of((2 * n + h) * LANES, LANES), LANES)
                natural[part, :, lanes] = wide[part, h, pl.ds(own + n, sources, stride=stride), :].astype(out.dtype)
        return 0

    pieces = PIECES if tile % PIECES == 0 else 1
    each = tile // pieces
    copies = []
    for piece in range(pieces):
        lax.fori_loop(piece * each, (piece + 1) * each, block, 0, unroll=8)
        lanes = pl.ds(piece * each * 2 * LANES, each * 2 * LANES)
        copies.append(pltpu.make_async_copy(natural.at[:, :, lanes], out.at[:, :, lanes], sems.at[piece]))
        copies[-1].start()
    for copy in copies:
        copy.wait()


def scalars_kernel(facts, sc):
    for i in range(sc.shape[0]):
        sc[i] = facts[i, 0]


IN_VMEM = pl.BlockSpec(memory_space=pltpu.VMEM)
IN_SMEM = pl.BlockSpec(memory_space=pltpu.SMEM)
IN_HBM = pl.BlockSpec(memory_space=pltpu.HBM)


def in_smem(a):
    return pltpu.with_memory_space_constraint(a, pltpu.SMEM)


def cost(size):
    return pl.CostEstimate(flops=0, bytes_accessed=size, transcendentals=0)


def per_device(source, pool, near_mask, layer_count):
    depth_n = lax.axis_size("depth")
    planes = lax.axis_size("plane")
    here = lax.axis_index("depth")
    plane = lax.axis_index("plane")
    cores = lax.axis_size("batch")
    cap = pool.shape[0]
    block = pool.shape[-1]
    sources = source.shape[2]
    tile = source.shape[3] // block
    blocks = tile * planes
    halo = min(4 * depth_n, tile) if planes == 2 else 4 * depth_n
    window = tile + halo if planes == 2 else min(blocks, tile + 2 * halo)
    start = jnp.clip(plane * tile - halo, 0, blocks - window)
    own = plane * tile - start
    chunks = sources
    rows = 2 * window
    params = pltpu.CompilerParams(vmem_limit_bytes=VMEM_LIMIT)
    bf16, f32 = jnp.bfloat16, jnp.float32

    facts = jnp.stack([here, layer_count[0], own]).astype(jnp.int32)
    facts = jnp.broadcast_to(jnp.pad(facts, (0, 5))[:, None], (8, LANES))
    cells = pltpu.with_memory_space_constraint(source[0], pltpu.HBM)
    weights = pltpu.with_memory_space_constraint(pool.reshape(cap, 3, 2 * block, block), pltpu.HBM)
    wide = pltpu.VMEM((2, 2, sources * (window + 1) + 8, LANES), f32)
    scalars = pltpu.SMEM((3,), jnp.int32)
    if planes == 2 and tile == LANES and 2 * cap <= sources:
        near = near_mask.transpose(0, 2, 1)
        head, payload, sc, near = pl.pallas_call(
            offer_kernel,
            out_shape=(
                pltpu.VMEM((2 * halo + 16, 2 * LANES), bf16),
                pltpu.VMEM((2, sources, halo * block), bf16),
                scalars,
                pltpu.VMEM(near.shape, near.dtype),
            ),
            in_specs=[IN_HBM, IN_HBM, IN_VMEM],
            out_specs=(IN_VMEM, IN_VMEM, IN_SMEM, IN_VMEM),
            scratch_shapes=[pltpu.VMEM((2 * halo + 16, 2 * LANES), f32), pltpu.SemaphoreType.DMA((2,))],
            compiler_params=params,
            cost_estimate=cost(1 << 20),
        )(cells, pltpu.with_memory_space_constraint(near, pltpu.HBM), held(facts))
        head = lax.ppermute(head, "plane", [(0, 1), (1, 0)])
        arrived = lax.ppermute(payload, "plane", [(0, 1), (1, 0)])
        src, mask, w = pl.pallas_call(
            enter_kernel,
            out_shape=(
                pltpu.VMEM((chunks, rows, block), bf16),
                pltpu.VMEM((cap, 2, window, LANES), f32),
                pltpu.VMEM(weights.shape, bf16),
            ),
            in_specs=[IN_HBM, IN_HBM, IN_VMEM, IN_SMEM],
            out_specs=(IN_VMEM,) * 3,
            scratch_shapes=[pltpu.VMEM(source.shape[1:], bf16), wide, pltpu.SemaphoreType.DMA((2,))],
            compiler_params=params,
            cost_estimate=cost(1 << 23),
        )(cells, weights, held(near), in_smem(sc))
        src, mask = pl.pallas_call(
            join_head_kernel,
            out_shape=(pltpu.VMEM(src.shape, bf16), pltpu.VMEM(mask.shape, f32)),
            in_specs=[IN_VMEM, IN_SMEM, IN_VMEM, IN_VMEM],
            out_specs=(IN_VMEM,) * 2,
            input_output_aliases={2: 0, 3: 1},
            compiler_params=params,
            cost_estimate=cost(1 << 18),
        )(held(head), in_smem(sc), held(src), held(mask))

        def complete(src):
            return pl.pallas_call(
                join_kernel,
                out_shape=pltpu.VMEM(src.shape, bf16),
                in_specs=[IN_VMEM, IN_SMEM, IN_VMEM],
                out_specs=IN_VMEM,
                input_output_aliases={2: 0},
                scratch_shapes=[wide],
                compiler_params=params,
                cost_estimate=cost(1 << 20),
            )(held(arrived), in_smem(sc), held(src))

    else:
        sc = pl.pallas_call(scalars_kernel, out_shape=scalars, in_specs=[IN_VMEM], out_specs=IN_SMEM)(held(facts))
        whole = lax.all_gather(source[0], "plane", axis=2, tiled=True)
        src = lax.dynamic_slice_in_dim(whole, start * block, window * block, axis=2)
        src = src.reshape(2, sources, window, block).transpose(1, 0, 2, 3).reshape(chunks, rows, block)
        present = lax.all_gather(near_mask, "plane", axis=1, tiled=True)
        present = lax.dynamic_slice_in_dim(present, start, window, axis=1).astype(f32)
        place = jnp.arange(window)[None, :]
        before = jnp.where(place == 0, 0.0, present[:, :, 0])
        after = jnp.where(place == window - 1, 0.0, present[:, :, 2])
        mask = jnp.broadcast_to(jnp.stack([before, after], axis=1)[..., None], (cap, 2, window, LANES))
        w = pool.reshape(cap, 3, 2 * block, block)
        complete = lambda src: src

    def swaps(first):
        pairs = [(i, i + 1) for i in range(first, depth_n - 1, 2)]
        alone = sorted(set(range(depth_n)) - {i for pair in pairs for i in pair})
        moves = [(i * cores + c, j * cores + c) for i, j in pairs for c in range(cores)]
        moves += [(i * cores + c, i * cores + c + 1) for i in alone for c in range(0, cores - 1, 2)]
        return moves + [(j, i) for i, j in moves]

    last_down = chunks + LAG * (depth_n - 1)
    first_up = LAG * (depth_n - 1)
    steps = chunks + 2 * LAG * (depth_n - 1)
    queue = [{}] * LAG
    kept = {}

    def leave(result):
        return pl.pallas_call(
            leave_kernel,
            out_shape=jax.ShapeDtypeStruct(source.shape[1:], bf16),
            in_specs=[IN_VMEM, IN_SMEM],
            out_specs=IN_HBM,
            scratch_shapes=[wide, pltpu.VMEM(source.shape[1:], bf16), pltpu.SemaphoreType.DMA((PIECES,))],
            compiler_params=params,
            cost_estimate=cost(1 << 22),
        )(held(result), in_smem(sc))[None]

    for step in range(steps):
        if step == steps - 1:
            kept["bottom"], kept["top"] = lax.optimization_barrier((kept["bottom"], kept["top"]))
            bottom = leave(kept["bottom"])
            bottom, kept["top"] = lax.optimization_barrier((bottom, kept["top"]))
        if step == 1:
            src = complete(src)
        if step == LAG:
            w = pl.pallas_call(
                turn_kernel,
                out_shape=pltpu.VMEM((cap, 3, block, 2 * block), bf16),
                in_specs=[IN_VMEM],
                out_specs=IN_VMEM,
                compiler_params=params,
                cost_estimate=cost(1 << 22),
            )(held(w))
        sends = {}
        if step < steps - LAG:
            sends["o1"] = ("r1", swaps(0))
        if LAG <= step < steps - 2 * LAG:
            sends["o2"] = ("r2", swaps(1))
        held_now = {"state": kept.get("state")}
        if step < last_down:
            held_now["bottom"] = kept.get("bottom")
        if step >= first_up:
            held_now["top"] = kept.get("top")
        out = section(depth_n, step, sc, dict(src=src, w=w, mask=mask), queue.pop(0), held_now, sends)
        queue.append({to: lax.ppermute(out.pop(name), ("depth", "batch"), pairs) for name, (to, pairs) in sends.items()})
        kept.update(out)

    return (leave(kept["top"]), bottom)


def solution(mesh):
    return jax.shard_map(
        per_device,
        mesh=mesh,
        in_specs=(
            P("depth", None, ("group", "batch"), "plane"),
            P("depth", None, None, None, None),
            P("depth", "plane", None),
            P("depth"),
        ),
        out_specs=(
            P("depth", None, ("group", "batch"), "plane"),
            P("depth", None, ("group", "batch"), "plane"),
        ),
        check_vma=False,
    )
```

```python
import functools

import jax
import jax.numpy as jnp
from jax import lax
from jax.experimental import pallas as pl
from jax.experimental.pallas import tpu as pltpu
from jax.sharding import PartitionSpec as P

NN = (((1,), (0,)), ((), ()))
NT = (((1,), (1,)), ((), ()))
CHUNKS = 8
LAG = 2
VMEM_LIMIT = 16 * 1024 * 1024


def apply_layer(x, w, mask, slot):
    rows, window = x.shape[0], mask.shape[2]
    half = rows // 2
    wide = x.astype(jnp.float32)
    before = pltpu.roll(wide, 1, 0) * jnp.tile(mask[slot, 0], (rows // window, 2))
    after = pltpu.roll(wide, rows - 1, 0) * jnp.tile(mask[slot, 1], (rows // window, 2))
    sides = (before.astype(jnp.bfloat16), x, after.astype(jnp.bfloat16))
    block = x.shape[1]
    if w.shape[2] == block:
        together = jnp.concatenate(sides, axis=1)
        turned = w[slot].reshape(3 * block, 2 * block)
        by_real = lax.dot_general(together, turned[:, :block], NN, preferred_element_type=jnp.float32)
        by_imag = lax.dot_general(together, turned[:, block:], NN, preferred_element_type=jnp.float32)
    else:
        total = sum(
            lax.dot_general(side, w[slot, i], NT, preferred_element_type=jnp.float32) for i, side in enumerate(sides)
        )
        by_real, by_imag = total[:, :block], total[:, block:]
    return by_real[:half] - by_imag[half:], by_real[half:] + by_imag[:half]


def section_kernel(depth_n, chunks, step, descends, plan, *refs):
    refs = dict(zip(plan, refs))
    sc, src, w, mask, state = (refs[name] for name in ("sc", "src", "w", "mask", "state"))
    here, count = sc[0], sc[1]
    down_at = step - LAG * here
    up_at = step - LAG * (2 * (depth_n - 1) - here)
    even = lax.rem(here, 2) == 0
    odd = jnp.logical_not(even)
    half = src.shape[1] // 2

    def choose(first, second, then):
        pl.when(even)(lambda: then(refs.get(first)))
        pl.when(odd)(lambda: then(refs.get(second)))

    def down():
        def enter(arrived):
            x = src[down_at]
            if arrived is None:
                state[down_at, 0] = x
                return

            @pl.when(here == 0)
            def _():
                state[down_at, 0] = x

            @pl.when(here > 0)
            def _():
                state[down_at, 0] = (arrived[...].astype(jnp.float32) + x.astype(jnp.float32)).astype(jnp.bfloat16)

        choose("r2", "r1", enter)

        def layer(c, _):
            real, imag = apply_layer(state[down_at, c], w, mask, c)
            state[down_at, c + 1, :half] = real.astype(jnp.bfloat16)
            state[down_at, c + 1, half:] = imag.astype(jnp.bfloat16)
            return 0

        lax.fori_loop(0, count, layer, 0)

        def send(out):
            if out is not None:
                out[...] = state[down_at, count]

        choose("o1", "o2", send)

    def rise():
        up = refs["up"]

        def enter(arrived):
            if arrived is not None:

                @pl.when(here < depth_n - 1)
                def _():
                    up[...] = arrived[...]

            @pl.when(here == depth_n - 1)
            def _():
                up[...] = jnp.zeros_like(up)

        choose("r1", "r2", enter)

        def layer(i, _):
            c = count - 1 - i
            real, imag = apply_layer(up[...], w, mask, c)
            up[:half] = (real + state[up_at, c, :half].astype(jnp.float32)).astype(jnp.bfloat16)
            up[half:] = (imag + state[up_at, c, half:].astype(jnp.float32)).astype(jnp.bfloat16)
            return 0

        lax.fori_loop(0, count, layer, 0)
        refs["top"][up_at] = up[...]

        def send(out):
            if out is not None:
                out[...] = up[...]

        choose("o2", "o1", send)

    if descends:
        pl.when((down_at >= 0) & (down_at < chunks))(down)
    if "top" in refs:
        pl.when((up_at >= 0) & (up_at < chunks))(rise)


def held(a):
    return pltpu.with_memory_space_constraint(a, pltpu.VMEM)


def section(depth_n, step, descends, sc, fixed, arrived, kept, sends):
    src = fixed["src"]
    chunks, rows, block = src.shape
    cap = fixed["w"].shape[0]
    in_vmem = pl.BlockSpec(memory_space=pltpu.VMEM)
    shapes = {"state": (chunks, cap + 1, rows, block), "top": src.shape}
    writes = ["state"] * descends + ["top"] * ("top" in kept)
    ins = {**fixed, **arrived, **{name: a for name, a in kept.items() if a is not None}}
    outs = writes + list(sends)
    aliases = {1 + list(ins).index(name): outs.index(name) for name in writes if name in ins}
    plan = ["sc"] + list(ins) + outs + ["up"]
    results = pl.pallas_call(
        functools.partial(section_kernel, depth_n, chunks, step, descends, plan),
        out_shape=tuple(pltpu.VMEM(shapes.get(name, (rows, block)), src.dtype) for name in outs),
        in_specs=[pl.BlockSpec(memory_space=pltpu.SMEM)] + [in_vmem] * len(ins),
        out_specs=(in_vmem,) * len(outs),
        scratch_shapes=[pltpu.VMEM((rows, block), src.dtype)],
        input_output_aliases=aliases,
        compiler_params=pltpu.CompilerParams(vmem_limit_bytes=VMEM_LIMIT),
        cost_estimate=pl.CostEstimate(
            flops=12 * rows * 6 * block * block, bytes_accessed=8 * rows * block, transcendentals=0
        ),
    )(pltpu.with_memory_space_constraint(sc, pltpu.SMEM), *map(held, ins.values()))
    return dict(zip(outs, results))


LANES = 128


def offer_kernel(source, near, facts, head, payload, sc, near_out, lines, sems):
    for i in range(sc.shape[0]):
        sc[i] = facts[i, 0]
    width = payload.shape[2]
    halo = width // (2 * LANES)
    first = jnp.where(facts[2, 0] == 0, source.shape[2] - width, 0)
    copy = pltpu.make_async_copy(source.at[:, :, pl.ds(pl.multiple_of(first, LANES), width)], payload, sems.at[0])
    bring = pltpu.make_async_copy(near, near_out, sems.at[1])
    copy.start()
    bring.start()
    lines[...] = jnp.zeros_like(lines)
    bring.wait()
    for slot in range(near.shape[0]):
        for side in range(2):
            at = 2 * halo + slot * 2 + side
            lines[at : at + 1, :LANES] = near_out[slot, 2 * side : 2 * side + 1, :].astype(jnp.float32)
    copy.wait()
    for part in range(2):
        for n in range(halo):
            at = part * halo + n
            lines[at : at + 1, :] = payload[part, 0:1, 2 * n * LANES : 2 * (n + 1) * LANES].astype(jnp.float32)
    head[...] = lines[...].astype(head.dtype)


def column(line):
    return jnp.broadcast_to(line, (LANES, LANES)).T


def enter_kernel(source, pool, near, sc, src, mask, w, natural, wide, sems):
    own = pl.multiple_of(sc[2], 16)
    bring = pltpu.make_async_copy(pool, w, sems.at[0])
    load = pltpu.make_async_copy(source, natural, sems.at[1])
    load.start()
    bring.start()
    sources = src.shape[0]
    window = mask.shape[2]
    tile = near.shape[2]
    for slot in range(mask.shape[0]):
        for side in range(2):
            mask[slot, side, pl.ds(own, tile), :] = column(near[slot, 2 * side : 2 * side + 1, :].astype(jnp.float32))
    load.wait()
    spread(natural, wide, own, tile, sources, window)
    for part in range(2):
        for s in range(sources):
            for h in range(2):
                src[s, pl.ds(part * window + own, tile), h * LANES : (h + 1) * LANES] = wide[
                    part, h, pl.ds(s * (window + 1) + own, tile), :
                ].astype(src.dtype)
    bring.wait()


def turn_kernel(w, turned):
    def turn(i, _):
        slot, offset = i // 3, lax.rem(i, 3)
        turned[slot, offset] = w[slot, offset].T
        return 0

    lax.fori_loop(0, w.shape[0] * 3, turn, 0)


def spread(natural, wide, first, count, sources, window):
    def block(n, _):
        for part in range(2):
            for h in range(2):
                lanes = pl.ds(pl.multiple_of((2 * n + h) * LANES, LANES), LANES)
                wide[part, h, pl.ds(first + n, sources, stride=window + 1), :] = natural[part, :, lanes].astype(
                    jnp.float32
                )
        return 0

    lax.fori_loop(0, count, block, 0, unroll=8)


def join_head_kernel(head, sc, src_in, mask_in, src, mask):
    own = sc[2]
    window = mask.shape[2]
    halo = (head.shape[0] - 16) // 2
    at = pl.multiple_of(jnp.where(own == 0, window - halo, 0), 16)
    for part in range(2):
        src[0, pl.ds(part * window + at, halo), :] = head[part * halo : (part + 1) * halo, :]
    for slot in range(mask.shape[0]):
        for side in range(2):
            r = 2 * halo + slot * 2 + side
            rows = column(head[r : r + 1, :LANES].astype(jnp.float32))
            mask[slot, side, pl.ds(at, halo), :] = jnp.where(own == 0, rows[:halo], rows[LANES - halo :])
            end = 0 if side == 0 else window - 1
            mask[slot, side, end : end + 1, :] = jnp.zeros((1, LANES), jnp.float32)


def join_kernel(arrived, sc, src_in, src, wide):
    own = sc[2]
    sources, window = src.shape[0], src.shape[1] // 2
    halo = arrived.shape[2] // (2 * LANES)
    at = pl.multiple_of(jnp.where(own == 0, window - halo, 0), 16)
    spread(arrived, wide, at, halo, sources, window)
    for part in range(2):
        for s in range(1, sources):
            for h in range(2):
                src[s, pl.ds(part * window + at, halo), h * LANES : (h + 1) * LANES] = wide[
                    part, h, pl.ds(s * (window + 1) + at, halo), :
                ].astype(src.dtype)


PIECES = 4


def leave_kernel(result, sc, out, wide, natural, sems):
    own = sc[2]
    sources, window = result.shape[0], result.shape[-2] // 2
    tile = out.shape[2] // (2 * LANES)
    stride = window + 1
    for part in range(2):
        for s in range(sources):
            for h in range(2):
                where = (s,) if len(result.shape) == 3 else (s, sc[1])
                wide[part, h, pl.ds(s * stride, window), :] = result[
                    (*where, pl.ds(part * window, window), slice(h * LANES, (h + 1) * LANES))
                ].astype(jnp.float32)

    def block(n, _):
        for part in range(2):
            for h in range(2):
                lanes = pl.ds(pl.multiple_of((2 * n + h) * LANES, LANES), LANES)
                natural[part, :, lanes] = wide[part, h, pl.ds(own + n, sources, stride=stride), :].astype(out.dtype)
        return 0

    pieces = PIECES if tile % PIECES == 0 else 1
    each = tile // pieces
    copies = []
    for piece in range(pieces):
        lax.fori_loop(piece * each, (piece + 1) * each, block, 0, unroll=8)
        lanes = pl.ds(piece * each * 2 * LANES, each * 2 * LANES)
        copies.append(pltpu.make_async_copy(natural.at[:, :, lanes], out.at[:, :, lanes], sems.at[piece]))
        copies[-1].start()
    for copy in copies:
        copy.wait()


def scalars_kernel(facts, sc):
    for i in range(sc.shape[0]):
        sc[i] = facts[i, 0]


IN_VMEM = pl.BlockSpec(memory_space=pltpu.VMEM)
IN_SMEM = pl.BlockSpec(memory_space=pltpu.SMEM)
IN_HBM = pl.BlockSpec(memory_space=pltpu.HBM)


def in_smem(a):
    return pltpu.with_memory_space_constraint(a, pltpu.SMEM)


def cost(size):
    return pl.CostEstimate(flops=0, bytes_accessed=size, transcendentals=0)


def per_device(source, pool, near_mask, layer_count):
    depth_n = lax.axis_size("depth")
    planes = lax.axis_size("plane")
    here = lax.axis_index("depth")
    plane = lax.axis_index("plane")
    cores = lax.axis_size("batch")
    cap = pool.shape[0]
    block = pool.shape[-1]
    sources = source.shape[2]
    tile = source.shape[3] // block
    blocks = tile * planes
    halo = min(4 * depth_n, tile) if planes == 2 else 4 * depth_n
    window = tile + halo if planes == 2 else min(blocks, tile + 2 * halo)
    start = jnp.clip(plane * tile - halo, 0, blocks - window)
    own = plane * tile - start
    chunks = sources
    rows = 2 * window
    params = pltpu.CompilerParams(vmem_limit_bytes=VMEM_LIMIT)
    bf16, f32 = jnp.bfloat16, jnp.float32

    facts = jnp.stack([here, layer_count[0], own]).astype(jnp.int32)
    facts = jnp.broadcast_to(jnp.pad(facts, (0, 5))[:, None], (8, LANES))
    cells = pltpu.with_memory_space_constraint(source[0], pltpu.HBM)
    weights = pltpu.with_memory_space_constraint(pool.reshape(cap, 3, 2 * block, block), pltpu.HBM)
    wide = pltpu.VMEM((2, 2, sources * (window + 1) + 8, LANES), f32)
    scalars = pltpu.SMEM((3,), jnp.int32)
    if planes == 2 and tile == LANES and 2 * cap <= sources:
        near = near_mask.transpose(0, 2, 1)
        head, payload, sc, near = pl.pallas_call(
            offer_kernel,
            out_shape=(
                pltpu.VMEM((2 * halo + 16, 2 * LANES), bf16),
                pltpu.VMEM((2, sources, halo * block), bf16),
                scalars,
                pltpu.VMEM(near.shape, near.dtype),
            ),
            in_specs=[IN_HBM, IN_HBM, IN_VMEM],
            out_specs=(IN_VMEM, IN_VMEM, IN_SMEM, IN_VMEM),
            scratch_shapes=[pltpu.VMEM((2 * halo + 16, 2 * LANES), f32), pltpu.SemaphoreType.DMA((2,))],
            compiler_params=params,
            cost_estimate=cost(1 << 20),
        )(cells, pltpu.with_memory_space_constraint(near, pltpu.HBM), held(facts))
        head = lax.ppermute(head, "plane", [(0, 1), (1, 0)])
        arrived = lax.ppermute(payload, "plane", [(0, 1), (1, 0)])
        src, mask, w = pl.pallas_call(
            enter_kernel,
            out_shape=(
                pltpu.VMEM((chunks, rows, block), bf16),
                pltpu.VMEM((cap, 2, window, LANES), f32),
                pltpu.VMEM(weights.shape, bf16),
            ),
            in_specs=[IN_HBM, IN_HBM, IN_VMEM, IN_SMEM],
            out_specs=(IN_VMEM,) * 3,
            scratch_shapes=[pltpu.VMEM(source.shape[1:], bf16), wide, pltpu.SemaphoreType.DMA((2,))],
            compiler_params=params,
            cost_estimate=cost(1 << 23),
        )(cells, weights, held(near), in_smem(sc))
        src, mask = pl.pallas_call(
            join_head_kernel,
            out_shape=(pltpu.VMEM(src.shape, bf16), pltpu.VMEM(mask.shape, f32)),
            in_specs=[IN_VMEM, IN_SMEM, IN_VMEM, IN_VMEM],
            out_specs=(IN_VMEM,) * 2,
            input_output_aliases={2: 0, 3: 1},
            compiler_params=params,
            cost_estimate=cost(1 << 18),
        )(held(head), in_smem(sc), held(src), held(mask))

        def complete(src):
            return pl.pallas_call(
                join_kernel,
                out_shape=pltpu.VMEM(src.shape, bf16),
                in_specs=[IN_VMEM, IN_SMEM, IN_VMEM],
                out_specs=IN_VMEM,
                input_output_aliases={2: 0},
                scratch_shapes=[wide],
                compiler_params=params,
                cost_estimate=cost(1 << 20),
            )(held(arrived), in_smem(sc), held(src))

    else:
        sc = pl.pallas_call(scalars_kernel, out_shape=scalars, in_specs=[IN_VMEM], out_specs=IN_SMEM)(held(facts))
        whole = lax.all_gather(source[0], "plane", axis=2, tiled=True)
        src = lax.dynamic_slice_in_dim(whole, start * block, window * block, axis=2)
        src = src.reshape(2, sources, window, block).transpose(1, 0, 2, 3).reshape(chunks, rows, block)
        present = lax.all_gather(near_mask, "plane", axis=1, tiled=True)
        present = lax.dynamic_slice_in_dim(present, start, window, axis=1).astype(f32)
        place = jnp.arange(window)[None, :]
        before = jnp.where(place == 0, 0.0, present[:, :, 0])
        after = jnp.where(place == window - 1, 0.0, present[:, :, 2])
        mask = jnp.broadcast_to(jnp.stack([before, after], axis=1)[..., None], (cap, 2, window, LANES))
        w = pool.reshape(cap, 3, 2 * block, block)
        complete = lambda src: src

    def swaps(first):
        pairs = [(i, i + 1) for i in range(first, depth_n - 1, 2)]
        alone = sorted(set(range(depth_n)) - {i for pair in pairs for i in pair})
        moves = [(i * cores + c, j * cores + c) for i, j in pairs for c in range(cores)]
        moves += [(i * cores + c, i * cores + c + 1) for i in alone for c in range(0, cores - 1, 2)]
        return moves + [(j, i) for i, j in moves]

    last_down = chunks + LAG * (depth_n - 1)
    first_up = LAG * (depth_n - 1)
    steps = chunks + 2 * LAG * (depth_n - 1)
    queue = [{}] * LAG
    kept = {}

    def leave(result):
        return pl.pallas_call(
            leave_kernel,
            out_shape=jax.ShapeDtypeStruct(source.shape[1:], bf16),
            in_specs=[IN_VMEM, IN_SMEM],
            out_specs=IN_HBM,
            scratch_shapes=[wide, pltpu.VMEM(source.shape[1:], bf16), pltpu.SemaphoreType.DMA((PIECES,))],
            compiler_params=params,
            cost_estimate=cost(1 << 22),
        )(held(result), in_smem(sc))[None]

    for step in range(steps):
        if step == steps - 1:
            kept = dict(zip(kept, lax.optimization_barrier(tuple(kept.values()))))
            bottom = leave(kept["state"])
            bottom, kept["top"] = lax.optimization_barrier((bottom, kept["top"]))
        if step == 1:
            src = complete(src)
        if step == LAG:
            w, kept["state"] = lax.optimization_barrier((w, kept["state"]))
            w = pl.pallas_call(
                turn_kernel,
                out_shape=pltpu.VMEM((cap, 3, block, 2 * block), bf16),
                in_specs=[IN_VMEM],
                out_specs=IN_VMEM,
                compiler_params=params,
                cost_estimate=cost(1 << 22),
            )(held(w))
        sends = {}
        if step < steps - LAG:
            sends["o1"] = ("r1", swaps(0))
        if LAG <= step < steps - 2 * LAG:
            sends["o2"] = ("r2", swaps(1))
        held_now = {"state": kept.get("state")}
        if step >= first_up:
            held_now["top"] = kept.get("top")
        out = section(depth_n, step, step < last_down, sc, dict(src=src, w=w, mask=mask), queue.pop(0), held_now, sends)
        queue.append({to: lax.ppermute(out.pop(name), ("depth", "batch"), pairs) for name, (to, pairs) in sends.items()})
        kept.update(out)

    return (leave(kept["top"]), bottom)


def solution(mesh):
    return jax.shard_map(
        per_device,
        mesh=mesh,
        in_specs=(
            P("depth", None, ("group", "batch"), "plane"),
            P("depth", None, None, None, None),
            P("depth", "plane", None),
            P("depth"),
        ),
        out_specs=(
            P("depth", None, ("group", "batch"), "plane"),
            P("depth", None, ("group", "batch"), "plane"),
        ),
        check_vma=False,
    )
```

```python
import functools

import jax
import jax.numpy as jnp
from jax import lax
from jax.experimental import pallas as pl
from jax.experimental.pallas import tpu as pltpu
from jax.sharding import PartitionSpec as P

NN = (((1,), (0,)), ((), ()))
NT = (((1,), (1,)), ((), ()))
CHUNKS = 8
LAG = 2
VMEM_LIMIT = 16 * 1024 * 1024


def apply_layer(x, w, mask, slot):
    rows, window = x.shape[0], mask.shape[2]
    half = rows // 2
    wide = x.astype(jnp.float32)
    before = pltpu.roll(wide, 1, 0) * jnp.tile(mask[slot, 0], (rows // window, 2))
    after = pltpu.roll(wide, rows - 1, 0) * jnp.tile(mask[slot, 1], (rows // window, 2))
    sides = (before.astype(jnp.bfloat16), x, after.astype(jnp.bfloat16))
    block = x.shape[1]
    if w.shape[2] == block:
        together = jnp.concatenate(sides, axis=1)
        turned = w[slot].reshape(3 * block, 2 * block)
        by_real = lax.dot_general(together, turned[:, :block], NN, preferred_element_type=jnp.float32)
        by_imag = lax.dot_general(together, turned[:, block:], NN, preferred_element_type=jnp.float32)
    else:
        total = sum(
            lax.dot_general(side, w[slot, i], NT, preferred_element_type=jnp.float32) for i, side in enumerate(sides)
        )
        by_real, by_imag = total[:, :block], total[:, block:]
    return by_real[:half] - by_imag[half:], by_real[half:] + by_imag[:half]


def section_kernel(depth_n, chunks, step, descends, plan, *refs):
    refs = dict(zip(plan, refs))
    sc, src, w, mask, state = (refs[name] for name in ("sc", "src", "w", "mask", "state"))
    here, count = sc[0], sc[1]
    down_at = step - LAG * here
    up_at = step - LAG * (2 * (depth_n - 1) - here)
    even = lax.rem(here, 2) == 0
    odd = jnp.logical_not(even)
    half = src.shape[1] // 2

    def choose(first, second, then):
        pl.when(even)(lambda: then(refs.get(first)))
        pl.when(odd)(lambda: then(refs.get(second)))

    def down():
        def enter(arrived):
            x = src[down_at]
            if arrived is None:
                state[down_at, 0] = x
                return

            @pl.when(here == 0)
            def _():
                state[down_at, 0] = x

            @pl.when(here > 0)
            def _():
                state[down_at, 0] = (arrived[...].astype(jnp.float32) + x.astype(jnp.float32)).astype(jnp.bfloat16)

        choose("r2", "r1", enter)

        def layer(c, _):
            real, imag = apply_layer(state[down_at, c], w, mask, c)
            state[down_at, c + 1, :half] = real.astype(jnp.bfloat16)
            state[down_at, c + 1, half:] = imag.astype(jnp.bfloat16)
            return 0

        lax.fori_loop(0, count, layer, 0)

        def send(out):
            if out is not None:
                out[...] = state[down_at, count]

        choose("o1", "o2", send)

    def rise():
        up = refs["up"]

        def enter(arrived):
            if arrived is not None:

                @pl.when(here < depth_n - 1)
                def _():
                    up[...] = arrived[...]

            @pl.when(here == depth_n - 1)
            def _():
                up[...] = jnp.zeros_like(up)

        choose("r1", "r2", enter)

        def layer(i, _):
            c = count - 1 - i
            real, imag = apply_layer(up[...], w, mask, c)
            up[:half] = (real + state[up_at, c, :half].astype(jnp.float32)).astype(jnp.bfloat16)
            up[half:] = (imag + state[up_at, c, half:].astype(jnp.float32)).astype(jnp.bfloat16)
            return 0

        lax.fori_loop(0, count, layer, 0)
        refs["top"][up_at] = up[...]

        def send(out):
            if out is not None:
                out[...] = up[...]

        choose("o2", "o1", send)

    if descends:
        pl.when((down_at >= 0) & (down_at < chunks))(down)
    if "top" in refs:
        pl.when((up_at >= 0) & (up_at < chunks))(rise)


def held(a):
    return pltpu.with_memory_space_constraint(a, pltpu.VMEM)


def section(depth_n, step, descends, sc, fixed, arrived, kept, sends):
    src = fixed["src"]
    chunks, rows, block = src.shape
    cap = fixed["w"].shape[0]
    in_vmem = pl.BlockSpec(memory_space=pltpu.VMEM)
    shapes = {"state": (chunks, cap + 1, rows, block), "top": src.shape}
    writes = ["state"] * descends + ["top"] * ("top" in kept)
    ins = {**fixed, **arrived, **{name: a for name, a in kept.items() if a is not None}}
    outs = writes + list(sends)
    aliases = {1 + list(ins).index(name): outs.index(name) for name in writes if name in ins}
    plan = ["sc"] + list(ins) + outs + ["up"]
    results = pl.pallas_call(
        functools.partial(section_kernel, depth_n, chunks, step, descends, plan),
        out_shape=tuple(pltpu.VMEM(shapes.get(name, (rows, block)), src.dtype) for name in outs),
        in_specs=[pl.BlockSpec(memory_space=pltpu.SMEM)] + [in_vmem] * len(ins),
        out_specs=(in_vmem,) * len(outs),
        scratch_shapes=[pltpu.VMEM((rows, block), src.dtype)],
        input_output_aliases=aliases,
        compiler_params=pltpu.CompilerParams(vmem_limit_bytes=VMEM_LIMIT),
        cost_estimate=pl.CostEstimate(
            flops=12 * rows * 6 * block * block, bytes_accessed=8 * rows * block, transcendentals=0
        ),
    )(pltpu.with_memory_space_constraint(sc, pltpu.SMEM), *map(held, ins.values()))
    return dict(zip(outs, results))


LANES = 128


PIECES = 4


def offer_kernel(source, near, facts, head, payload, sc, near_out, lines, sems):
    for i in range(sc.shape[0]):
        sc[i] = facts[i, 0]
    width = payload.shape[2]
    halo = width // (2 * LANES)
    first = jnp.where(facts[2, 0] == 0, source.shape[2] - width, 0)
    copy = pltpu.make_async_copy(source.at[:, :, pl.ds(pl.multiple_of(first, LANES), width)], payload, sems.at[0])
    bring = pltpu.make_async_copy(near, near_out, sems.at[1])
    copy.start()
    bring.start()
    lines[...] = jnp.zeros_like(lines)
    bring.wait()
    for slot in range(near.shape[0]):
        for side in range(2):
            at = 2 * halo + slot * 2 + side
            lines[at : at + 1, :LANES] = near_out[slot, 2 * side : 2 * side + 1, :].astype(jnp.float32)
    copy.wait()
    for part in range(2):
        for n in range(halo):
            at = part * halo + n
            lines[at : at + 1, :] = payload[part, 0:1, 2 * n * LANES : 2 * (n + 1) * LANES].astype(jnp.float32)
    head[...] = lines[...].astype(head.dtype)


def column(line):
    return jnp.broadcast_to(line, (LANES, LANES)).T


def enter_kernel(source, pool, near, sc, src, mask, w, natural, wide, sems):
    own = pl.multiple_of(sc[2], 16)
    each = source.shape[2] // PIECES
    loads = []
    for piece in range(PIECES):
        lanes = pl.ds(piece * each, each)
        loads.append(pltpu.make_async_copy(source.at[:, :, lanes], natural.at[:, :, lanes], sems.at[piece]))
        loads[-1].start()
    bring = pltpu.make_async_copy(pool, w, sems.at[PIECES])
    bring.start()
    sources = src.shape[0]
    window = mask.shape[2]
    tile = near.shape[2]
    for slot in range(mask.shape[0]):
        for side in range(2):
            mask[slot, side, pl.ds(own, tile), :] = column(near[slot, 2 * side : 2 * side + 1, :].astype(jnp.float32))
    for piece in range(PIECES):
        loads[piece].wait()
        count = tile // PIECES
        spread(natural, wide, own, piece * count, count, sources, window)
    for part in range(2):
        for s in range(sources):
            for h in range(2):
                src[s, pl.ds(part * window + own, tile), h * LANES : (h + 1) * LANES] = wide[
                    part, h, pl.ds(s * (window + 1) + own, tile), :
                ].astype(src.dtype)
    bring.wait()


def turn_kernel(w, turned):
    def turn(i, _):
        slot, offset = i // 3, lax.rem(i, 3)
        turned[slot, offset] = w[slot, offset].T
        return 0

    lax.fori_loop(0, w.shape[0] * 3, turn, 0)


def spread(natural, wide, first, begin, count, sources, window):
    def block(n, _):
        for part in range(2):
            for h in range(2):
                lanes = pl.ds(pl.multiple_of((2 * n + h) * LANES, LANES), LANES)
                wide[part, h, pl.ds(first + n, sources, stride=window + 1), :] = natural[part, :, lanes].astype(
                    jnp.float32
                )
        return 0

    lax.fori_loop(begin, begin + count, block, 0, unroll=8)


def join_head_kernel(head, sc, src_in, mask_in, src, mask):
    own = sc[2]
    window = mask.shape[2]
    halo = (head.shape[0] - 16) // 2
    at = pl.multiple_of(jnp.where(own == 0, window - halo, 0), 16)
    for part in range(2):
        src[0, pl.ds(part * window + at, halo), :] = head[part * halo : (part + 1) * halo, :]
    for slot in range(mask.shape[0]):
        for side in range(2):
            r = 2 * halo + slot * 2 + side
            rows = column(head[r : r + 1, :LANES].astype(jnp.float32))
            mask[slot, side, pl.ds(at, halo), :] = jnp.where(own == 0, rows[:halo], rows[LANES - halo :])
            end = 0 if side == 0 else window - 1
            mask[slot, side, end : end + 1, :] = jnp.zeros((1, LANES), jnp.float32)


def join_kernel(arrived, sc, src_in, src, wide):
    own = sc[2]
    sources, window = src.shape[0], src.shape[1] // 2
    halo = arrived.shape[2] // (2 * LANES)
    at = pl.multiple_of(jnp.where(own == 0, window - halo, 0), 16)
    spread(arrived, wide, at, 0, halo, sources, window)
    for part in range(2):
        for s in range(1, sources):
            for h in range(2):
                src[s, pl.ds(part * window + at, halo), h * LANES : (h + 1) * LANES] = wide[
                    part, h, pl.ds(s * (window + 1) + at, halo), :
                ].astype(src.dtype)


def leave_kernel(result, sc, out, wide, natural, sems):
    own = sc[2]
    sources, window = result.shape[0], result.shape[-2] // 2
    tile = out.shape[2] // (2 * LANES)
    stride = window + 1
    for part in range(2):
        for s in range(sources):
            for h in range(2):
                where = (s,) if len(result.shape) == 3 else (s, sc[1])
                wide[part, h, pl.ds(s * stride, window), :] = result[
                    (*where, pl.ds(part * window, window), slice(h * LANES, (h + 1) * LANES))
                ].astype(jnp.float32)

    def block(n, _):
        for part in range(2):
            for h in range(2):
                lanes = pl.ds(pl.multiple_of((2 * n + h) * LANES, LANES), LANES)
                natural[part, :, lanes] = wide[part, h, pl.ds(own + n, sources, stride=stride), :].astype(out.dtype)
        return 0

    pieces = PIECES if tile % PIECES == 0 else 1
    each = tile // pieces
    copies = []
    for piece in range(pieces):
        lax.fori_loop(piece * each, (piece + 1) * each, block, 0, unroll=8)
        lanes = pl.ds(piece * each * 2 * LANES, each * 2 * LANES)
        copies.append(pltpu.make_async_copy(natural.at[:, :, lanes], out.at[:, :, lanes], sems.at[piece]))
        copies[-1].start()
    for copy in copies:
        copy.wait()


def scalars_kernel(facts, sc):
    for i in range(sc.shape[0]):
        sc[i] = facts[i, 0]


IN_VMEM = pl.BlockSpec(memory_space=pltpu.VMEM)
IN_SMEM = pl.BlockSpec(memory_space=pltpu.SMEM)
IN_HBM = pl.BlockSpec(memory_space=pltpu.HBM)


def in_smem(a):
    return pltpu.with_memory_space_constraint(a, pltpu.SMEM)


def cost(size):
    return pl.CostEstimate(flops=0, bytes_accessed=size, transcendentals=0)


def per_device(source, pool, near_mask, layer_count):
    depth_n = lax.axis_size("depth")
    planes = lax.axis_size("plane")
    here = lax.axis_index("depth")
    plane = lax.axis_index("plane")
    cores = lax.axis_size("batch")
    cap = pool.shape[0]
    block = pool.shape[-1]
    sources = source.shape[2]
    tile = source.shape[3] // block
    blocks = tile * planes
    halo = min(4 * depth_n, tile) if planes == 2 else 4 * depth_n
    window = tile + halo if planes == 2 else min(blocks, tile + 2 * halo)
    start = jnp.clip(plane * tile - halo, 0, blocks - window)
    own = plane * tile - start
    chunks = sources
    rows = 2 * window
    params = pltpu.CompilerParams(vmem_limit_bytes=VMEM_LIMIT)
    bf16, f32 = jnp.bfloat16, jnp.float32

    facts = jnp.stack([here, layer_count[0], own]).astype(jnp.int32)
    facts = jnp.broadcast_to(jnp.pad(facts, (0, 5))[:, None], (8, LANES))
    cells = pltpu.with_memory_space_constraint(source[0], pltpu.HBM)
    weights = pltpu.with_memory_space_constraint(pool.reshape(cap, 3, 2 * block, block), pltpu.HBM)
    wide = pltpu.VMEM((2, 2, sources * (window + 1) + 8, LANES), f32)
    scalars = pltpu.SMEM((3,), jnp.int32)
    if planes == 2 and tile == LANES and 2 * cap <= sources:
        near = near_mask.transpose(0, 2, 1)
        head, payload, sc, near = pl.pallas_call(
            offer_kernel,
            out_shape=(
                pltpu.VMEM((2 * halo + 16, 2 * LANES), bf16),
                pltpu.VMEM((2, sources, halo * block), bf16),
                scalars,
                pltpu.VMEM(near.shape, near.dtype),
            ),
            in_specs=[IN_HBM, IN_HBM, IN_VMEM],
            out_specs=(IN_VMEM, IN_VMEM, IN_SMEM, IN_VMEM),
            scratch_shapes=[pltpu.VMEM((2 * halo + 16, 2 * LANES), f32), pltpu.SemaphoreType.DMA((2,))],
            compiler_params=params,
            cost_estimate=cost(1 << 20),
        )(cells, pltpu.with_memory_space_constraint(near, pltpu.HBM), held(facts))
        head = lax.ppermute(head, "plane", [(0, 1), (1, 0)])
        arrived = lax.ppermute(payload, "plane", [(0, 1), (1, 0)])
        src, mask, w = pl.pallas_call(
            enter_kernel,
            out_shape=(
                pltpu.VMEM((chunks, rows, block), bf16),
                pltpu.VMEM((cap, 2, window, LANES), f32),
                pltpu.VMEM(weights.shape, bf16),
            ),
            in_specs=[IN_HBM, IN_HBM, IN_VMEM, IN_SMEM],
            out_specs=(IN_VMEM,) * 3,
            scratch_shapes=[pltpu.VMEM(source.shape[1:], bf16), wide, pltpu.SemaphoreType.DMA((PIECES + 1,))],
            compiler_params=params,
            cost_estimate=cost(1 << 23),
        )(cells, weights, held(near), in_smem(sc))
        src, mask = pl.pallas_call(
            join_head_kernel,
            out_shape=(pltpu.VMEM(src.shape, bf16), pltpu.VMEM(mask.shape, f32)),
            in_specs=[IN_VMEM, IN_SMEM, IN_VMEM, IN_VMEM],
            out_specs=(IN_VMEM,) * 2,
            input_output_aliases={2: 0, 3: 1},
            compiler_params=params,
            cost_estimate=cost(1 << 18),
        )(held(head), in_smem(sc), held(src), held(mask))

        def complete(src):
            return pl.pallas_call(
                join_kernel,
                out_shape=pltpu.VMEM(src.shape, bf16),
                in_specs=[IN_VMEM, IN_SMEM, IN_VMEM],
                out_specs=IN_VMEM,
                input_output_aliases={2: 0},
                scratch_shapes=[wide],
                compiler_params=params,
                cost_estimate=cost(1 << 20),
            )(held(arrived), in_smem(sc), held(src))

    else:
        sc = pl.pallas_call(scalars_kernel, out_shape=scalars, in_specs=[IN_VMEM], out_specs=IN_SMEM)(held(facts))
        whole = lax.all_gather(source[0], "plane", axis=2, tiled=True)
        src = lax.dynamic_slice_in_dim(whole, start * block, window * block, axis=2)
        src = src.reshape(2, sources, window, block).transpose(1, 0, 2, 3).reshape(chunks, rows, block)
        present = lax.all_gather(near_mask, "plane", axis=1, tiled=True)
        present = lax.dynamic_slice_in_dim(present, start, window, axis=1).astype(f32)
        place = jnp.arange(window)[None, :]
        before = jnp.where(place == 0, 0.0, present[:, :, 0])
        after = jnp.where(place == window - 1, 0.0, present[:, :, 2])
        mask = jnp.broadcast_to(jnp.stack([before, after], axis=1)[..., None], (cap, 2, window, LANES))
        w = pool.reshape(cap, 3, 2 * block, block)
        complete = lambda src: src

    def swaps(first):
        pairs = [(i, i + 1) for i in range(first, depth_n - 1, 2)]
        alone = sorted(set(range(depth_n)) - {i for pair in pairs for i in pair})
        moves = [(i * cores + c, j * cores + c) for i, j in pairs for c in range(cores)]
        moves += [(i * cores + c, i * cores + c + 1) for i in alone for c in range(0, cores - 1, 2)]
        return moves + [(j, i) for i, j in moves]

    last_down = chunks + LAG * (depth_n - 1)
    first_up = LAG * (depth_n - 1)
    steps = chunks + 2 * LAG * (depth_n - 1)
    queue = [{}] * LAG
    kept = {}

    def leave(result):
        return pl.pallas_call(
            leave_kernel,
            out_shape=jax.ShapeDtypeStruct(source.shape[1:], bf16),
            in_specs=[IN_VMEM, IN_SMEM],
            out_specs=IN_HBM,
            scratch_shapes=[wide, pltpu.VMEM(source.shape[1:], bf16), pltpu.SemaphoreType.DMA((PIECES,))],
            compiler_params=params,
            cost_estimate=cost(1 << 22),
        )(held(result), in_smem(sc))[None]

    for step in range(steps):
        if step == steps - 1:
            kept = dict(zip(kept, lax.optimization_barrier(tuple(kept.values()))))
            bottom = leave(kept["state"])
            bottom, kept["top"] = lax.optimization_barrier((bottom, kept["top"]))
        if step == 1:
            src = complete(src)
        if step == LAG:
            w, kept["state"] = lax.optimization_barrier((w, kept["state"]))
            w = pl.pallas_call(
                turn_kernel,
                out_shape=pltpu.VMEM((cap, 3, block, 2 * block), bf16),
                in_specs=[IN_VMEM],
                out_specs=IN_VMEM,
                compiler_params=params,
                cost_estimate=cost(1 << 22),
            )(held(w))
        sends = {}
        if step < steps - LAG:
            sends["o1"] = ("r1", swaps(0))
        if LAG <= step < steps - 2 * LAG:
            sends["o2"] = ("r2", swaps(1))
        held_now = {"state": kept.get("state")}
        if step >= first_up:
            held_now["top"] = kept.get("top")
        out = section(depth_n, step, step < last_down, sc, dict(src=src, w=w, mask=mask), queue.pop(0), held_now, sends)
        queue.append({to: lax.ppermute(out.pop(name), ("depth", "batch"), pairs) for name, (to, pairs) in sends.items()})
        kept.update(out)

    return (leave(kept["top"]), bottom)


def solution(mesh):
    return jax.shard_map(
        per_device,
        mesh=mesh,
        in_specs=(
            P("depth", None, ("group", "batch"), "plane"),
            P("depth", None, None, None, None),
            P("depth", "plane", None),
            P("depth"),
        ),
        out_specs=(
            P("depth", None, ("group", "batch"), "plane"),
            P("depth", None, ("group", "batch"), "plane"),
        ),
        check_vma=False,
    )
```
